256 devices in a mesh: blocks: 64 (over z, x, core), section: 4 (over y).
Axes of the slice: x: 4, y: 4, z: 8, core: 2. Of those that a mesh axis runs over, the one named last changes fastest.
Arguments:
- features: bfloat16 [256, 32, 4096], P(('blocks', 'section')), may hold values from -6 to 6
- grad_pool: bfloat16 [256, 32, 4096], P(('blocks', 'section')), may hold values from -6 to 6
- grad_skip: bfloat16 [256, 32, 4096], P(('blocks', 'section')), may hold values from -6 to 6
- conv_one: bfloat16 [27, 32, 32], replicated, may hold values from -0.21875 to 0.21875
- conv_two: bfloat16 [27, 32, 32], replicated, may hold values from -0.21875 to 0.21875
- block_links: int32 [256, 6], P(('blocks', 'section')), may hold values from -1 to 255, as said below
- block_positions: int32 [256, 3], P(('blocks', 'section')), may hold values from 0 to 4095
- dropout_seed: int32 [1], replicated, may hold values from 0 to 1048575
Outputs:
- encoded: bfloat16 [256, 32, 4096], P(('blocks', 'section'))
- grad_features: bfloat16 [256, 32, 4096], P(('blocks', 'section'))
- grad_conv_one: float32 [27, 32, 32], replicated
- grad_conv_two: float32 [27, 32, 32], replicated
The draws below stay inside these ranges and needn't reach their ends.
Inputs may be any that keep to these rules, and one draw needn't show every extreme that they name: `block_links`: links are mutual: if entry 2k+1 (the + face along axis k) of block a is b, then entry 2k of block b is a, and the reverse. A block never names itself, and every block named is held by the same device as the naming block or by the device one index before or after it along blocks+section, the last and the first device counting as neighbours.
All inputs are finite; a program needn't handle non-finite values.
Results may differ from the reference program's by a relative error of at most 0.0059.
Values may be sent and summed in bfloat16 or wider, within the bound.
A program may use at most 192 MiB of HBM per device.

```python
import jax
import jax.numpy as jnp
from jax import lax

C = 32
EDGE = 16
BPD = 1
BLOCKS = 256


def window_order(key, groups, width, half):
    ruler = jnp.arange(width, dtype=jnp.int32)
    first_slot = jax.random.randint(jax.random.fold_in(key, 1), (groups,), 0, half, dtype=jnp.int32)
    last_slot = half + jax.random.randint(jax.random.fold_in(key, 2), (groups,), 0, half, dtype=jnp.int32)
    scores = jax.random.randint(jax.random.fold_in(key, 3), (groups, width), 0, 1 << 20, dtype=jnp.int32) * width + ruler[None, :]
    scores = jnp.where(ruler[None, :] == first_slot[:, None], -1, scores)
    scores = jnp.where(ruler[None, :] == last_slot[:, None], (1 << 20) * width + width, scores)
    return jnp.argsort(scores, axis=1).astype(jnp.int32)


def draw_block_links(key, part):
    key = jax.random.fold_in(key, 5)
    whole = BLOCKS
    width = 2 * BPD
    groups = whole // width
    ruler = jnp.arange(whole, dtype=jnp.int32)
    labels = jax.random.randint(jax.random.fold_in(key, 1), (whole,), 0, 6, dtype=jnp.int32)
    rotation = jax.random.randint(jax.random.fold_in(key, 2), (), 0, whole, dtype=jnp.int32)
    labels = labels.at[(rotation + whole - 1) % whole].set(0)
    labels = labels.at[rotation].set(3)
    labels = labels.at[(rotation + 1) % whole].set(0)
    following = (ruler + 1) % whole
    preceding = (ruler + whole - 1) % whole
    columns = []
    for axis_id in range(3):
        offset = BPD if axis_id == 1 else 0
        sequence = window_order(jax.random.fold_in(key, 30 + axis_id), groups, width, BPD)
        inverse = jnp.argsort(sequence, axis=1).astype(jnp.int32)
        shifted = (ruler - offset + whole) % whole
        group_id = shifted // width
        within = shifted % width
        block_at = (group_id * width + sequence[group_id, within] + offset) % whole
        position_of = (group_id * width + inverse[group_id, within] + offset) % whole
        severed = (labels == axis_id).astype(jnp.int32)
        linked = severed == 0
        passed = jnp.cumsum(severed) - severed
        inner_total = passed[whole - 1]
        segment = jnp.where((passed == inner_total) & (severed[whole - 1] == 0), 0, passed).astype(jnp.int32)
        directions = jax.random.randint(jax.random.fold_in(key, 10 + axis_id), (whole,), 0, 2, dtype=jnp.int32)
        heading = directions[segment]
        twinned = jax.random.randint(jax.random.fold_in(key, 20 + axis_id), (whole,), 0, 2, dtype=jnp.int32)
        if axis_id == 0:
            twinned = twinned.at[rotation].set(1)
            twinned = twinned.at[(rotation + whole - 2) % whole].set(0)
        paired = linked & (severed[preceding] == 1) & (severed[following] == 1) & (twinned == 1)
        prev_linked = linked[preceding]
        prev_heading = heading[preceding]
        plus_side = jnp.where(linked & (heading == 0), following, jnp.where(prev_linked & (prev_heading == 1), preceding, -1))
        minus_side = jnp.where(linked & (heading == 1), following, jnp.where(prev_linked & (prev_heading == 0), preceding, -1))
        plus_side = jnp.where(paired, following, jnp.where(paired[preceding], preceding, plus_side))
        minus_side = jnp.where(paired, following, jnp.where(paired[preceding], preceding, minus_side))
        plus_block = jnp.where(plus_side >= 0, block_at[jnp.maximum(plus_side, 0)], -1)
        minus_block = jnp.where(minus_side >= 0, block_at[jnp.maximum(minus_side, 0)], -1)
        columns.append(minus_block[position_of].astype(jnp.int32))
        columns.append(plus_block[position_of].astype(jnp.int32))
    return jnp.stack(columns, axis=1)


def with_ends(array, own_key, low, largest):
    longest = array.shape.index(max(array.shape))
    spots = []
    for shift in (0, 1):
        where = [jax.random.randint(jax.random.fold_in(own_key, axis), (), 0, length) for axis, length in enumerate(array.shape)]
        where[longest] = (where[longest] + shift) % array.shape[longest]
        spots.append(tuple(where))
    return array.at[spots[0]].set(low).at[spots[1]].set(largest)


def shard_levels(key, extent, cuts, low, top_value):
    level = 1.0
    for dim, parts in cuts:
        steps = jax.random.uniform(jax.random.fold_in(jax.random.fold_in(key, 6), dim), (parts,), jnp.float32, low / len(cuts), top_value / len(cuts))
        level = level * jnp.repeat(jnp.exp(steps), extent[dim] // parts).reshape((-1,) + (1,) * (len(extent) - 1 - dim))
    return level


def gaussian(own_key, dims, spread, reach, split=(), held_as=jnp.bfloat16):
    values = jax.random.normal(own_key, dims, jnp.float32) * spread
    if len(split) > 0:
        values = shard_levels(own_key, dims, split, -0.22, 0.18) * values
    return jnp.clip(values, min=-reach, max=reach).astype(held_as)


def setup_inputs(seed: int = 0) -> dict:
    streams_of = jax.random.split(jax.random.key(seed), 9)
    return {
        "features": gaussian(streams_of[0], (BLOCKS, C, EDGE**3), 1.0, 6.0, ((0, 256),)),
        "grad_pool": gaussian(streams_of[1], (BLOCKS, C, EDGE**3), 1.0, 6.0, ((0, 256),)),
        "grad_skip": gaussian(streams_of[2], (BLOCKS, C, EDGE**3), 1.0, 6.0, ((0, 256),)),
        "conv_one": gaussian(streams_of[3], (27, C, C), (27 * C) ** -0.5, 0.21875),
        "conv_two": gaussian(streams_of[4], (27, C, C), (27 * C) ** -0.5, 0.21875),
        "block_links": draw_block_links(jax.random.fold_in(streams_of[8], 71), 0),
        "block_positions": with_ends(jax.random.randint(streams_of[6], (BLOCKS, 3), 0, 4096), jax.random.fold_in(streams_of[6], 1), 0, 4095).astype(jnp.int32),
        "dropout_seed": jax.random.randint(streams_of[7], (1,), 0, 1048576).astype(jnp.int32),
    }


keep_factor = 1024.0 / 819.0

def face_layers(block_cube):
    number = block_cube.shape[0]
    planes = [block_cube[:, :, 0], block_cube[:, :, -1], block_cube[:, :, :, 0], block_cube[:, :, :, -1], block_cube[:, :, :, :, 0], block_cube[:, :, :, :, -1]]
    return jnp.stack(planes, axis=1).reshape(number, 6, C, EDGE * EDGE)

def gather_rims(layers, block_links):
    opposite = jnp.bitwise_xor(jnp.arange(6, dtype=jnp.int32), 1)[None, :]
    safe_links = jnp.maximum(block_links, 0).astype(jnp.int32)
    picked = layers[safe_links, opposite]
    return jnp.where((block_links >= 0)[:, :, None, None], picked, jnp.zeros_like(picked))

def extend(block_cube, rim_layers):
    number = block_cube.shape[0]
    sheets = rim_layers.reshape(number, 6, C, EDGE, EDGE)
    padded = jnp.pad(block_cube, ((0, 0), (0, 0), (1, 1), (1, 1), (1, 1)))
    middle = slice(1, EDGE + 1)
    padded = padded.at[:, :, 0, middle, middle].set(sheets[:, 0])
    padded = padded.at[:, :, EDGE + 1, middle, middle].set(sheets[:, 1])
    padded = padded.at[:, :, middle, 0, middle].set(sheets[:, 2])
    padded = padded.at[:, :, middle, EDGE + 1, middle].set(sheets[:, 3])
    padded = padded.at[:, :, middle, middle, 0].set(sheets[:, 4])
    padded = padded.at[:, :, middle, middle, EDGE + 1].set(sheets[:, 5])
    return padded

def window_at(padded, offset):
    shift_x, shift_y, shift_z = (offset // 9, offset // 3 % 3, offset % 3)
    number = padded.shape[0]
    window = padded[:, :, shift_x:shift_x + EDGE, shift_y:shift_y + EDGE, shift_z:shift_z + EDGE]
    return window.reshape(number, C, EDGE ** 3)

def convolve(padded, kernel):
    number = padded.shape[0]
    summed = jnp.zeros((number, C, EDGE ** 3), jnp.float32)
    for offset in range(27):
        window = window_at(padded, offset)
        summed = summed + jnp.einsum('oc,ncv->nov', kernel[offset].astype(jnp.float32), window.astype(jnp.float32))
    return summed

def weight_grad(upstream, padded):
    pieces = []
    for offset in range(27):
        window = window_at(padded, offset)
        pieces.append(jnp.einsum('nov,ncv->oc', upstream.astype(jnp.float32), window.astype(jnp.float32)))
    return jnp.stack(pieces, axis=0)

def mirrored_kernel(kernel):
    return jnp.transpose(kernel[::-1], (0, 2, 1))

def keep_scale(block_positions, dropout_seed):
    number = block_positions.shape[0]
    ruler = jnp.arange(EDGE, dtype=jnp.int32)
    global_x = block_positions[:, 0][:, None, None, None, None] * EDGE + ruler[None, None, :, None, None]
    global_y = block_positions[:, 1][:, None, None, None, None] * EDGE + ruler[None, None, None, :, None]
    global_z = block_positions[:, 2][:, None, None, None, None] * EDGE + ruler[None, None, None, None, :]
    channel = jnp.arange(C, dtype=jnp.int32)[None, :, None, None, None]
    hashed = jnp.bitwise_xor(global_x * jnp.int32(73856093), global_y * jnp.int32(19349663))
    hashed = jnp.bitwise_xor(hashed, global_z * jnp.int32(83492791))
    hashed = jnp.bitwise_xor(hashed, channel * jnp.int32(1103515245))
    hashed = jnp.bitwise_xor(hashed, dropout_seed[0] * jnp.int32(668265263))
    hashed = jnp.bitwise_xor(hashed, lax.shift_right_logical(hashed, jnp.int32(13)))
    hashed = hashed * jnp.int32(1274126177)
    hashed = jnp.bitwise_xor(hashed, lax.shift_right_logical(hashed, jnp.int32(16)))
    kept_mask = jnp.bitwise_and(hashed, jnp.int32(1023)) >= 205
    scale = jnp.where(kept_mask, jnp.float32(keep_factor), jnp.float32(0.0))
    return scale.reshape(number, C, EDGE ** 3)

def reference(features, grad_pool, grad_skip, conv_one, conv_two, block_links, block_positions, dropout_seed):
    number = features.shape[0]
    shape_cube = (number, C, EDGE, EDGE, EDGE)
    norm_factor = 1.0 / jnp.sqrt(jnp.float32(number * EDGE ** 3))
    input_cube = features.reshape(shape_cube)
    padded_in = extend(input_cube, gather_rims(face_layers(input_cube), block_links))
    pre = convolve(padded_in, conv_one)
    keep = keep_scale(block_positions, dropout_seed)
    dropped = (jax.nn.silu(pre) * keep).astype(jnp.bfloat16)
    dropped_cube = dropped.reshape(shape_cube)
    padded_drop = extend(dropped_cube, gather_rims(face_layers(dropped_cube), block_links))
    encoded = convolve(padded_drop, conv_two).astype(jnp.bfloat16)
    upstream = (grad_pool.astype(jnp.float32) + grad_skip.astype(jnp.float32)).astype(jnp.bfloat16)
    grad_conv_two = weight_grad(upstream, padded_drop) * norm_factor
    upstream_cube = upstream.reshape(shape_cube)
    padded_up = extend(upstream_cube, gather_rims(face_layers(upstream_cube), block_links))
    back = convolve(padded_up, mirrored_kernel(conv_two))
    logistic = jax.nn.sigmoid(pre)
    inner = (back * keep * logistic * (1.0 + pre * (1.0 - logistic))).astype(jnp.bfloat16)
    grad_conv_one = weight_grad(inner, padded_in) * norm_factor
    inner_cube = inner.reshape(shape_cube)
    padded_inner = extend(inner_cube, gather_rims(face_layers(inner_cube), block_links))
    grad_features = convolve(padded_inner, mirrored_kernel(conv_one)).astype(jnp.bfloat16)
    return (encoded, grad_features, grad_conv_one, grad_conv_two)
```

```python
import functools
import math

import jax
import jax.numpy as jnp
import numpy as np
from jax import lax
from jax.experimental import pallas as pl
from jax.experimental.pallas import tpu as pltpu
from jax.sharding import PartitionSpec as P

C = 32
EDGE = 16
PLANE = EDGE * EDGE
SLABS = EDGE + 2
KEEP = 1024.0 / 819.0
MESH = pl.DeviceIdType.MESH
BF = jnp.bfloat16
F32 = jnp.float32

SHIFTS = [s for s in range(9) if s != 4] + [4]
PLACE = {s: i for i, s in enumerate(SHIFTS)}


def shift_matrices():
    table = np.zeros((PLANE + 128, 8 * PLANE), np.float32)
    for i, s in enumerate(SHIFTS[:8]):
        dy, dz = s // 3 - 1, s % 3 - 1
        for y in range(EDGE):
            for z in range(EDGE):
                column = i * PLANE + y * EDGE + z
                sy, sz = y + dy, z + dz
                in_y, in_z = 0 <= sy < EDGE, 0 <= sz < EDGE
                if in_y and in_z:
                    table[sy * EDGE + sz, column] = 1
                elif in_z:
                    slot = 0 if sy < 0 else 1
                    for half in (0, 64):
                        table[PLANE + half + slot * EDGE + sz, column] = 1
                elif in_y:
                    slot = 2 if sz < 0 else 3
                    for half in (0, 64):
                        table[PLANE + half + slot * EDGE + sy, column] = 1
    return table


def face_matrix():
    table = np.zeros((2 * PLANE, 128), np.float32)
    for half in (0, 1):
        for i in range(EDGE):
            base = half * 64
            table[half * PLANE + (EDGE - 1) * EDGE + i, base + i] = 1
            table[half * PLANE + i, base + EDGE + i] = 1
            table[half * PLANE + i * EDGE + EDGE - 1, base + 2 * EDGE + i] = 1
            table[half * PLANE + i * EDGE, base + 3 * EDGE + i] = 1
    return table


def dot(a, b):
    return jnp.dot(a, b, preferred_element_type=F32)


def dot_nt(a, b):
    return lax.dot_general(a, b, (((1,), (1,)), ((), ())), preferred_element_type=F32)


def kernel(
    count,
    feat_ref,
    pool_ref,
    skip_ref,
    one_ref,
    two_ref,
    shift_ref,
    face_ref,
    links_ref,
    pos_ref,
    seed_ref,
    enc_ref,
    gfeat_ref,
    gone_ref,
    gtwo_ref,
    v_f,
    v_u,
    v_d,
    v_i,
    im_f,
    im_u,
    im_d,
    im_i,
    w_one,
    w_two,
    wt_one,
    wt_two,
    y_buf,
    z_buf,
    keep_buf,
    d_all,
    i_all,
    sendf,
    recvp,
    recvn,
    g_full,
    g_send,
    g_slots,
    z_slots,
    r_send,
    fin,
    fsend_sem,
    frecv_sem,
    s1_send,
    s1_recv,
    s2_send,
    s2_recv,
    s3_send,
    s3_recv,
):
    blocks, section = lax.axis_index("blocks"), lax.axis_index("section")
    per = lax.axis_size("section")
    me = blocks * per + section
    group = 32
    rings = count // group
    ring, rank = me // group, lax.rem(me, group)

    def at(index):
        return (index // per, lax.rem(index, per))

    nxt = lax.rem(me + 1, count)
    prv = lax.rem(me + count - 1, count)

    barrier = pltpu.get_barrier_semaphore()
    for d in (prv, nxt):
        pl.semaphore_signal(barrier, inc=1, device_id=at(d), device_id_type=MESH)

    def greet_group(o, carry):
        t = ring * group + lax.rem(rank + o, group)
        pl.semaphore_signal(barrier, inc=1, device_id=at(t), device_id_type=MESH)
        return carry

    lax.fori_loop(1, group, greet_group, 0)

    def greet_ring(o, carry):
        t = lax.rem(ring + o, rings) * group + rank
        pl.semaphore_signal(barrier, inc=1, device_id=at(t), device_id_type=MESH)
        return carry

    lax.fori_loop(1, rings, greet_ring, 0)

    for x in range(EDGE):
        rows, lanes = pl.ds((x + 1) * C, C), pl.ds(x * PLANE, PLANE)
        v_f[rows, 0:PLANE] = feat_ref[0, :, lanes]
        v_u[rows, 0:PLANE] = (
            pool_ref[0, :, lanes].astype(F32) + skip_ref[0, :, lanes].astype(F32)
        ).astype(BF)
    zero = jnp.zeros((C, 128), BF)
    for v in (v_f, v_u, v_d, v_i):
        v[0:C, PLANE:] = zero
        v[(SLABS - 1) * C :, PLANE:] = zero

    inner_rows = pl.ds(C, EDGE * C)

    def pack_faces(v, slot):
        last = EDGE * C
        sendf[slot, 0:32, :] = v[last : last + C, 0:128]
        sendf[slot, 32:64, :] = v[last : last + C, 128:256]
        sendf[slot, 64:96, :] = v[C : 2 * C, 0:128]
        sendf[slot, 96:128, :] = v[C : 2 * C, 128:256]
        packed = dot(v[C : 9 * C, 0:PLANE], face_ref[0:PLANE, :]) + dot(
            v[9 * C : 17 * C, 0:PLANE], face_ref[PLANE:, :]
        )
        sendf[slot, 128:384, :] = packed.astype(BF)

    def face_copies(slot):
        to_next = pltpu.make_async_remote_copy(
            src_ref=sendf.at[slot],
            dst_ref=recvp.at[slot],
            send_sem=fsend_sem.at[2 * slot],
            recv_sem=frecv_sem.at[2 * slot],
            device_id=at(nxt),
            device_id_type=MESH,
        )
        to_prev = pltpu.make_async_remote_copy(
            src_ref=sendf.at[slot],
            dst_ref=recvn.at[slot],
            send_sem=fsend_sem.at[2 * slot + 1],
            recv_sem=frecv_sem.at[2 * slot + 1],
            device_id=at(prv),
            device_id_type=MESH,
        )
        return to_next, to_prev

    def send_faces(slot):
        copies = face_copies(slot)
        for copy in copies:
            copy.start()
        return copies

    pack_faces(v_f, 0)
    pack_faces(v_u, 1)
    pl.semaphore_wait(barrier, 2 + (group - 1) + (rings - 1))
    sent = [send_faces(0), send_faces(1)]

    def weights(ref, plain, mirrored):
        for k in range(3):
            plain[k * C : (k + 1) * C, :] = jnp.concatenate(
                [ref[k * 9 + s].astype(F32) for s in SHIFTS], axis=1
            ).astype(BF)
        stacked = jnp.concatenate(
            [
                jnp.concatenate(
                    [ref[26 - (k * 9 + s)].astype(F32) for k in range(3)]
                    + [jnp.zeros((C, C), F32)],
                    axis=1,
                )
                for s in SHIFTS
            ]
            + [jnp.zeros((96, 128), F32)],
            axis=0,
        )
        mirrored[...] = jnp.transpose(stacked)[0:96, 0:288].astype(BF)

    weights(one_ref, w_one, wt_one)
    weights(two_ref, w_two, wt_two)

    lane = lax.broadcasted_iota(jnp.int32, (C, PLANE), 1)
    channel = lax.broadcasted_iota(jnp.int32, (C, PLANE), 0)
    base = (pos_ref[0, 1] * EDGE + lax.shift_right_logical(lane, 4)) * jnp.int32(19349663)
    base = base ^ ((pos_ref[0, 2] * EDGE + (lane & 15)) * jnp.int32(83492791))
    base = base ^ (channel * jnp.int32(1103515245))
    base = base ^ (seed_ref[0] * jnp.int32(668265263))
    for x in range(EDGE):
        h = base ^ ((pos_ref[0, 0] * EDGE + x) * jnp.int32(73856093))
        h = h ^ lax.shift_right_logical(h, 13)
        h = h * jnp.int32(1274126177)
        h = h ^ lax.shift_right_logical(h, 16)
        keep_buf[x * C : (x + 1) * C, :] = jnp.where((h & 1023) >= 205, F32(KEEP), F32(0.0))

    for k in range(3):
        for j in range(SLABS):
            if not 0 <= j - k < EDGE:
                for ref in (d_all, i_all):
                    ref[k * C : (k + 1) * C, j * PLANE : (j + 1) * PLANE] = jnp.zeros(
                        (C, PLANE), BF
                    )

    def shift_here(v, im):
        for x in range(EDGE):
            im[8 * C :, (x + 1) * PLANE : (x + 2) * PLANE] = v[(x + 1) * C : (x + 2) * C, 0:PLANE]
        for i in range(8):
            moved = dot(v[inner_rows, 0:PLANE], shift_ref[0:PLANE, i * PLANE : (i + 1) * PLANE])
            for x in range(EDGE):
                im[i * C : (i + 1) * C, (x + 1) * PLANE : (x + 2) * PLANE] = moved[
                    x * C : (x + 1) * C
                ].astype(BF)

    shift_here(v_f, im_f)
    shift_here(v_u, im_u)

    mlane = lax.broadcasted_iota(jnp.int32, (16, 128), 1)
    slot_of = lax.shift_right_logical(mlane, 4) & 3
    wanted = jnp.full((16, 128), -1, jnp.int32)
    for k in range(4):
        wanted = jnp.where(slot_of == k, links_ref[0, 2 + k], wanted)

    def weight_of(condition):
        return jnp.where(condition, F32(1.0), F32(0.0)).astype(BF)[0:1, :]

    low = mlane < 64
    p_low = weight_of((wanted == prv) & low)
    n_low = weight_of((wanted == nxt) & low)
    p_high = weight_of((wanted == prv) & (mlane >= 64))
    n_high = weight_of((wanted == nxt) & (mlane >= 64))
    x_masks = []
    for k in range(2):
        link = jnp.full((16, 128), links_ref[0, k], jnp.int32)
        x_masks.append((weight_of(link == prv), weight_of(link == nxt)))

    def take_rims(v, im, slot):
        for k in range(2):
            mp, mn = x_masks[k]
            row = 0 if k == 0 else (SLABS - 1) * C
            for half in range(2):
                at_rows = pl.ds(k * 64 + half * 32, 32)
                v[row : row + C, half * 128 : half * 128 + 128] = (
                    recvp[slot, at_rows, :] * mp + recvn[slot, at_rows, :] * mn
                )
        from_p, from_n = recvp[slot, 128:384, :], recvn[slot, 128:384, :]
        v[C : 9 * C, PLANE:] = from_p * p_low + from_n * n_low
        v[9 * C : 17 * C, PLANE:] = from_p * p_high + from_n * n_high
        for j in (0, SLABS - 1):
            rows, lanes = pl.ds(j * C, C), pl.ds(j * PLANE, PLANE)
            im[8 * C :, lanes] = v[rows, 0:PLANE]
        for i in range(8):
            rim = dot(v[inner_rows, PLANE:], shift_ref[PLANE:, i * PLANE : (i + 1) * PLANE])
            for x in range(EDGE):
                rows, lanes = pl.ds(i * C, C), pl.ds((x + 1) * PLANE, PLANE)
                im[rows, lanes] = im[rows, lanes] + rim[x * C : (x + 1) * C].astype(BF)
            for j in (0, SLABS - 1):
                im[i * C : (i + 1) * C, j * PLANE : (j + 1) * PLANE] = dot(
                    v[j * C : (j + 1) * C, 0:PLANE], shift_ref[0:PLANE, i * PLANE : (i + 1) * PLANE]
                ).astype(BF)

    def convolve(w, im, out):
        for j in range(0, SLABS, 2):
            lanes = pl.ds(j * PLANE, 2 * PLANE)
            out[:, lanes] = dot(w[...], im[:, lanes])

    def summed(y, x):
        return (
            y[0:C, x * PLANE : (x + 1) * PLANE]
            + y[C : 2 * C, (x + 1) * PLANE : (x + 2) * PLANE]
            + y[2 * C : 3 * C, (x + 2) * PLANE : (x + 3) * PLANE]
        )

    def arrive(slot):
        for copy in sent[slot]:
            copy.wait_recv()

    arrive(0)
    take_rims(v_f, im_f, 0)
    convolve(w_one, im_f, y_buf)
    for x in range(EDGE):
        pre = summed(y_buf, x)
        value = (jax.nn.silu(pre) * keep_buf[x * C : (x + 1) * C, :]).astype(BF)
        v_d[(x + 1) * C : (x + 2) * C, 0:PLANE] = value
        for k in range(3):
            d_all[k * C : (k + 1) * C, (x + k) * PLANE : (x + k + 1) * PLANE] = value
    pack_faces(v_d, 2)
    sent.append(send_faces(2))

    arrive(1)
    take_rims(v_u, im_u, 1)
    convolve(wt_two, im_u, z_buf)
    for x in range(EDGE):
        pre = summed(y_buf, x)
        back = summed(z_buf, x)
        logistic = jax.nn.sigmoid(pre)
        keep = keep_buf[x * C : (x + 1) * C, :]
        value = (back * keep * logistic * (1.0 + pre * (1.0 - logistic))).astype(BF)
        v_i[(x + 1) * C : (x + 2) * C, 0:PLANE] = value
        for k in range(3):
            i_all[k * C : (k + 1) * C, (x + k) * PLANE : (x + k + 1) * PLANE] = value
    pack_faces(v_i, 3)
    sent.append(send_faces(3))

    g_two = dot_nt(im_u[...], d_all[...])
    g_full[0:288, 0:96] = g_two
    g_full[0:288, 96:128] = jnp.zeros((288, 32), F32)
    g_one = dot_nt(i_all[...], im_f[...])
    g_full[288:384, :] = g_one[:, 0:128]
    g_full[384:480, :] = g_one[:, 128:256]
    g_full[480:512, :] = jnp.concatenate(
        [g_one[k * C : (k + 1) * C, 256:288] for k in range(3)] + [jnp.zeros((C, C), F32)], axis=1
    )
    g_send[...] = g_full[...].astype(BF)

    def chunk(index):
        return pl.ds(pl.multiple_of(index * 16, 16), 16)

    def scatter_copy(o):
        t = lax.rem(rank + o, group)
        return pltpu.make_async_remote_copy(
            src_ref=g_send.at[chunk(t), :],
            dst_ref=g_slots.at[o],
            send_sem=s1_send.at[o],
            recv_sem=s1_recv.at[o],
            device_id=at(ring * group + t),
            device_id_type=MESH,
        )

    def ring_copy(o):
        t = lax.rem(ring + o, rings)
        return pltpu.make_async_remote_copy(
            src_ref=z_slots.at[ring],
            dst_ref=z_slots.at[ring],
            send_sem=s2_send.at[o],
            recv_sem=s2_recv.at[o],
            device_id=at(t * group + rank),
            device_id_type=MESH,
        )

    def gather_copy(o):
        t = lax.rem(rank + o, group)
        return pltpu.make_async_remote_copy(
            src_ref=r_send,
            dst_ref=fin.at[chunk(rank), :],
            send_sem=s3_send.at[o],
            recv_sem=s3_recv.at[o],
            device_id=at(ring * group + t),
            device_id_type=MESH,
        )

    def each(copy_of, upto, act):
        def step(o, carry):
            act(copy_of(o))
            return carry

        lax.fori_loop(1, upto, step, 0)

    each(scatter_copy, group, lambda c: c.start())

    shift_here(v_d, im_d)

    each(scatter_copy, group, lambda c: c.wait_recv())
    total = g_full[chunk(rank), :]
    for o in range(1, group):
        total = total + g_slots[o].astype(F32)
    z_slots[ring] = total
    each(ring_copy, rings, lambda c: c.start())

    shift_here(v_i, im_i)

    arrive(2)
    take_rims(v_d, im_d, 2)
    convolve(w_two, im_d, y_buf)
    for x in range(EDGE):
        enc_ref[0, :, x * PLANE : (x + 1) * PLANE] = summed(y_buf, x).astype(BF)

    each(ring_copy, rings, lambda c: c.wait_recv())
    total = z_slots[0]
    for o in range(1, rings):
        total = total + z_slots[o]
    r_send[...] = total.astype(BF)
    fin[chunk(rank), :] = total.astype(BF)
    each(gather_copy, group, lambda c: c.start())

    arrive(3)
    take_rims(v_i, im_i, 3)
    convolve(wt_one, im_i, z_buf)
    for x in range(EDGE):
        gfeat_ref[0, :, x * PLANE : (x + 1) * PLANE] = summed(z_buf, x).astype(BF)

    each(gather_copy, group, lambda c: c.wait_recv())
    norm = F32(1.0 / math.sqrt(count * EDGE**3))
    for k in range(3):
        for s in range(9):
            p, q = PLACE[s], PLACE[8 - s]
            if p < 8:
                top, left = 288 + 96 * (p // 4) + k * C, (p % 4) * C
            else:
                top, left = 480, k * C
            rows = fin[top : top + C, :].astype(F32)
            gone_ref[k * 9 + s] = rows[:, left : left + C] * norm
            rows = fin[q * C : (q + 1) * C, :].astype(F32)
            gtwo_ref[k * 9 + s] = rows[:, (2 - k) * C : (3 - k) * C] * norm

    for pair in sent:
        for copy in pair:
            copy.wait_send()
    each(scatter_copy, group, lambda c: c.wait_send())
    each(ring_copy, rings, lambda c: c.wait_send())
    each(gather_copy, group, lambda c: c.wait_send())


def local(count, *args):
    features, pool, skip, one, two, links, positions, seed = args
    shift = jnp.asarray(shift_matrices(), BF)
    face = jnp.asarray(face_matrix(), BF)
    vmem = pl.BlockSpec(memory_space=pltpu.VMEM)
    smem = pl.BlockSpec(memory_space=pltpu.SMEM)
    rows, lanes = SLABS * C, SLABS * PLANE
    dma = pltpu.SemaphoreType.DMA
    rings = count // 32
    return pl.pallas_call(
        functools.partial(kernel, count),
        out_shape=(
            jax.ShapeDtypeStruct((1, C, EDGE**3), BF),
            jax.ShapeDtypeStruct((1, C, EDGE**3), BF),
            jax.ShapeDtypeStruct((27, C, C), F32),
            jax.ShapeDtypeStruct((27, C, C), F32),
        ),
        in_specs=[vmem] * 7 + [smem] * 3,
        out_specs=(vmem,) * 4,
        scratch_shapes=[pltpu.VMEM((rows, PLANE + 128), BF)] * 4
        + [pltpu.VMEM((9 * C, lanes), BF)] * 4
        + [pltpu.VMEM((96, 288), BF)] * 4
        + [pltpu.VMEM((96, lanes), F32)] * 2
        + [pltpu.VMEM((EDGE * C, PLANE), F32)]
        + [pltpu.VMEM((96, lanes), BF)] * 2
        + [pltpu.VMEM((4, 384, 128), BF)] * 3
        + [
            pltpu.VMEM((512, 128), F32),
            pltpu.VMEM((512, 128), BF),
            pltpu.VMEM((32, 16, 128), BF),
            pltpu.VMEM((rings, 16, 128), F32),
            pltpu.VMEM((16, 128), BF),
            pltpu.VMEM((512, 128), BF),
            dma((8,)),
            dma((8,)),
            dma((32,)),
            dma((32,)),
            dma((rings,)),
            dma((rings,)),
            dma((32,)),
            dma((32,)),
        ],
        compiler_params=pltpu.CompilerParams(
            collective_id=0, has_side_effects=True, vmem_limit_bytes=48 * 2**20
        ),
        cost_estimate=pl.CostEstimate(
            flops=4_000_000_000, bytes_accessed=3_000_000, transcendentals=300_000
        ),
    )(features, pool, skip, one, two, shift, face, links, positions, seed)


def solution(mesh):
    both = ("blocks", "section")
    in_specs = (
        P(both, None, None),
        P(both, None, None),
        P(both, None, None),
        P(),
        P(),
        P(both, None),
        P(both, None),
        P(),
    )
    out_specs = (P(both, None, None), P(both, None, None), P(), P())
    return jax.shard_map(
        functools.partial(local, mesh.size),
        mesh=mesh,
        in_specs=in_specs,
        out_specs=out_specs,
        check_vma=False,
    )
```

```python
import functools
import math

import jax
import jax.numpy as jnp
import numpy as np
from jax import lax
from jax.experimental import pallas as pl
from jax.experimental.pallas import tpu as pltpu
from jax.sharding import PartitionSpec as P

C = 32
EDGE = 16
PLANE = EDGE * EDGE
SLABS = EDGE + 2
KEEP = 1024.0 / 819.0
MESH = pl.DeviceIdType.MESH
BF = jnp.bfloat16
F32 = jnp.float32

SHIFTS = [s for s in range(9) if s != 4] + [4]
PLACE = {s: i for i, s in enumerate(SHIFTS)}


def shift_matrices():
    table = np.zeros((PLANE + 128, 8 * PLANE), np.float32)
    for i, s in enumerate(SHIFTS[:8]):
        dy, dz = s // 3 - 1, s % 3 - 1
        for y in range(EDGE):
            for z in range(EDGE):
                column = i * PLANE + y * EDGE + z
                sy, sz = y + dy, z + dz
                in_y, in_z = 0 <= sy < EDGE, 0 <= sz < EDGE
                if in_y and in_z:
                    table[sy * EDGE + sz, column] = 1
                elif in_z:
                    slot = 0 if sy < 0 else 1
                    for half in (0, 64):
                        table[PLANE + half + slot * EDGE + sz, column] = 1
                elif in_y:
                    slot = 2 if sz < 0 else 3
                    for half in (0, 64):
                        table[PLANE + half + slot * EDGE + sy, column] = 1
    return table


def face_matrix():
    table = np.zeros((2 * PLANE, 128), np.float32)
    for half in (0, 1):
        for i in range(EDGE):
            base = half * 64
            table[half * PLANE + (EDGE - 1) * EDGE + i, base + i] = 1
            table[half * PLANE + i, base + EDGE + i] = 1
            table[half * PLANE + i * EDGE + EDGE - 1, base + 2 * EDGE + i] = 1
            table[half * PLANE + i * EDGE, base + 3 * EDGE + i] = 1
    return table


def dot(a, b):
    return jnp.dot(a, b, preferred_element_type=F32)


def dot_nt(a, b):
    return lax.dot_general(a, b, (((1,), (1,)), ((), ())), preferred_element_type=F32)


def kernel(
    count,
    feat_hbm,
    pool_hbm,
    skip_hbm,
    one_hbm,
    two_hbm,
    shift_hbm,
    face_hbm,
    links_hbm,
    pos_hbm,
    seed_hbm,
    enc_hbm,
    gfeat_hbm,
    fin_hbm,
    enc_ref,
    gfeat_ref,
    feat_ref,
    pool_ref,
    skip_ref,
    one_ref,
    two_ref,
    shift_ref,
    face_ref,
    links_ref,
    pos_ref,
    seed_ref,
    v_f,
    v_u,
    v_d,
    v_i,
    im_f,
    im_u,
    im_d,
    im_i,
    w_one,
    w_two,
    wt_one,
    wt_two,
    c_one,
    c_two,
    ct_one,
    ct_two,
    y_buf,
    z_buf,
    keep_buf,
    pre_buf,
    d_all,
    i_all,
    sendf,
    recvp,
    recvn,
    g_full,
    g_send,
    g_slots,
    z_slots,
    r_send,
    fin,
    in_sem,
    out_sem,
    fsend_sem,
    frecv_sem,
    s1_send,
    s1_recv,
    s2_send,
    s2_recv,
    s3_send,
    s3_recv,
):
    blocks, section = lax.axis_index("blocks"), lax.axis_index("section")
    per = lax.axis_size("section")
    me = blocks * per + section
    group = 32
    rings = count // group
    ring, rank = me // group, lax.rem(me, group)

    def at(index):
        return (index // per, lax.rem(index, per))

    nxt = lax.rem(me + 1, count)
    prv = lax.rem(me + count - 1, count)

    loads = {}
    for i, (name, src, dst) in enumerate(
        [
            ("feat", feat_hbm, feat_ref),
            ("face", face_hbm, face_ref),
            ("pool", pool_hbm, pool_ref),
            ("skip", skip_hbm, skip_ref),
            ("shift", shift_hbm, shift_ref),
            ("one", one_hbm, one_ref),
            ("two", two_hbm, two_ref),
            ("links", links_hbm, links_ref),
            ("pos", pos_hbm, pos_ref),
            ("seed", seed_hbm, seed_ref),
        ]
    ):
        loads[name] = pltpu.make_async_copy(src, dst, in_sem.at[i])
        loads[name].start()

    barrier = pltpu.get_barrier_semaphore()
    for d in (prv, nxt):
        pl.semaphore_signal(barrier, inc=1, device_id=at(d), device_id_type=MESH)

    for o in range(1, group):
        t = ring * group + lax.rem(rank + o, group)
        pl.semaphore_signal(barrier, inc=1, device_id=at(t), device_id_type=MESH)
    for o in range(1, rings):
        t = lax.rem(ring + o, rings) * group + rank
        pl.semaphore_signal(barrier, inc=1, device_id=at(t), device_id_type=MESH)

    loads["feat"].wait()
    for x in range(EDGE):
        rows, lanes = pl.ds((x + 1) * C, C), pl.ds(x * PLANE, PLANE)
        v_f[rows, 0:PLANE] = feat_ref[0, :, lanes]
    loads["pool"].wait()
    loads["skip"].wait()
    for x in range(EDGE):
        rows, lanes = pl.ds((x + 1) * C, C), pl.ds(x * PLANE, PLANE)
        v_u[rows, 0:PLANE] = (
            pool_ref[0, :, lanes].astype(F32) + skip_ref[0, :, lanes].astype(F32)
        ).astype(BF)
    zero = jnp.zeros((C, 128), BF)
    for v in (v_f, v_u, v_d, v_i):
        v[0:C, PLANE:] = zero
        v[(SLABS - 1) * C :, PLANE:] = zero

    inner_rows = pl.ds(C, EDGE * C)

    def pack_faces(v, slot):
        last = EDGE * C
        sendf[slot, 0:32, :] = v[last : last + C, 0:128]
        sendf[slot, 32:64, :] = v[last : last + C, 128:256]
        sendf[slot, 64:96, :] = v[C : 2 * C, 0:128]
        sendf[slot, 96:128, :] = v[C : 2 * C, 128:256]
        packed = dot(v[C : 9 * C, 0:PLANE], face_ref[0:PLANE, :]) + dot(
            v[9 * C : 17 * C, 0:PLANE], face_ref[PLANE:, :]
        )
        sendf[slot, 128:384, :] = packed.astype(BF)

    def face_copies(slot):
        to_next = pltpu.make_async_remote_copy(
            src_ref=sendf.at[slot],
            dst_ref=recvp.at[slot],
            send_sem=fsend_sem.at[2 * slot],
            recv_sem=frecv_sem.at[2 * slot],
            device_id=at(nxt),
            device_id_type=MESH,
        )
        to_prev = pltpu.make_async_remote_copy(
            src_ref=sendf.at[slot],
            dst_ref=recvn.at[slot],
            send_sem=fsend_sem.at[2 * slot + 1],
            recv_sem=frecv_sem.at[2 * slot + 1],
            device_id=at(prv),
            device_id_type=MESH,
        )
        return to_next, to_prev

    def send_faces(slot):
        copies = face_copies(slot)
        for copy in copies:
            copy.start()
        return copies

    loads["face"].wait()
    pack_faces(v_f, 0)
    pack_faces(v_u, 1)
    pl.semaphore_wait(barrier, 2 + (group - 1) + (rings - 1))
    sent = [send_faces(0), send_faces(1)]

    for name in ("one", "two", "links", "pos", "seed", "shift"):
        loads[name].wait()

    def weights(ref, plain, mirrored, centre, mirrored_centre):
        for k in range(3):
            plain[k * C : (k + 1) * C, :] = jnp.concatenate(
                [ref[k * 9 + s].astype(F32) for s in SHIFTS[:8]], axis=1
            ).astype(BF)
        centre[...] = jnp.concatenate(
            [ref[k * 9 + 4].astype(F32) for k in range(3)], axis=1
        ).astype(BF)
        stacked = jnp.concatenate(
            [
                jnp.concatenate(
                    [ref[26 - (k * 9 + s)].astype(F32) for k in range(3)]
                    + [jnp.zeros((C, C), F32)],
                    axis=1,
                )
                for s in SHIFTS
            ]
            + [jnp.zeros((96, 128), F32)],
            axis=0,
        )
        turned = jnp.transpose(stacked)
        mirrored[...] = turned[0:96, 0:256].astype(BF)
        mirrored_centre[...] = jnp.concatenate(
            [turned[k * C : (k + 1) * C, 256:288] for k in range(3)], axis=1
        ).astype(BF)

    weights(one_ref, w_one, wt_one, c_one, ct_one)
    weights(two_ref, w_two, wt_two, c_two, ct_two)

    lane = lax.broadcasted_iota(jnp.int32, (C, PLANE), 1)
    channel = lax.broadcasted_iota(jnp.int32, (C, PLANE), 0)
    base = (pos_ref[0, 1] * EDGE + lax.shift_right_logical(lane, 4)) * jnp.int32(19349663)
    base = base ^ ((pos_ref[0, 2] * EDGE + (lane & 15)) * jnp.int32(83492791))
    base = base ^ (channel * jnp.int32(1103515245))
    base = base ^ (seed_ref[0] * jnp.int32(668265263))
    for x in range(EDGE):
        h = base ^ ((pos_ref[0, 0] * EDGE + x) * jnp.int32(73856093))
        h = h ^ lax.shift_right_logical(h, 13)
        h = h * jnp.int32(1274126177)
        h = h ^ lax.shift_right_logical(h, 16)
        keep_buf[x * C : (x + 1) * C, :] = jnp.where((h & 1023) >= 205, F32(KEEP), F32(0.0))

    for k in range(3):
        for j in range(SLABS):
            if not 0 <= j - k < EDGE:
                for ref in (d_all, i_all):
                    ref[k * C : (k + 1) * C, j * PLANE : (j + 1) * PLANE] = jnp.zeros(
                        (C, PLANE), BF
                    )

    def shift_here(v, im):
        for i in range(8):
            moved = dot(v[inner_rows, 0:PLANE], shift_ref[0:PLANE, i * PLANE : (i + 1) * PLANE])
            for x in range(EDGE):
                im[i * C : (i + 1) * C, (x + 1) * PLANE : (x + 2) * PLANE] = moved[
                    x * C : (x + 1) * C
                ].astype(BF)

    shift_here(v_f, im_f)
    shift_here(v_u, im_u)

    mlane = lax.broadcasted_iota(jnp.int32, (16, 128), 1)
    slot_of = lax.shift_right_logical(mlane, 4) & 3
    wanted = jnp.full((16, 128), -1, jnp.int32)
    for k in range(4):
        wanted = jnp.where(slot_of == k, links_ref[0, 2 + k], wanted)

    def weight_of(condition):
        return jnp.where(condition, F32(1.0), F32(0.0)).astype(BF)[0:1, :]

    low = mlane < 64
    p_low = weight_of((wanted == prv) & low)
    n_low = weight_of((wanted == nxt) & low)
    p_high = weight_of((wanted == prv) & (mlane >= 64))
    n_high = weight_of((wanted == nxt) & (mlane >= 64))
    x_masks = []
    for k in range(2):
        link = jnp.full((16, 128), links_ref[0, k], jnp.int32)
        x_masks.append((weight_of(link == prv), weight_of(link == nxt)))

    def take_rims(v, im, slot):
        for k in range(2):
            mp, mn = x_masks[k]
            row = 0 if k == 0 else (SLABS - 1) * C
            for half in range(2):
                at_rows = pl.ds(k * 64 + half * 32, 32)
                v[row : row + C, half * 128 : half * 128 + 128] = (
                    recvp[slot, at_rows, :] * mp + recvn[slot, at_rows, :] * mn
                )
        from_p, from_n = recvp[slot, 128:384, :], recvn[slot, 128:384, :]
        v[C : 9 * C, PLANE:] = from_p * p_low + from_n * n_low
        v[9 * C : 17 * C, PLANE:] = from_p * p_high + from_n * n_high
        outer = jnp.concatenate([v[0:C, 0:PLANE], v[(SLABS - 1) * C :, 0:PLANE]], axis=0)
        for i in range(8):
            rim = dot(v[inner_rows, PLANE:], shift_ref[PLANE:, i * PLANE : (i + 1) * PLANE])
            for x in range(EDGE):
                rows, lanes = pl.ds(i * C, C), pl.ds((x + 1) * PLANE, PLANE)
                im[rows, lanes] = im[rows, lanes] + rim[x * C : (x + 1) * C].astype(BF)
            ends = dot(outer, shift_ref[0:PLANE, i * PLANE : (i + 1) * PLANE]).astype(BF)
            im[i * C : (i + 1) * C, 0:PLANE] = ends[0:C]
            im[i * C : (i + 1) * C, (SLABS - 1) * PLANE :] = ends[C : 2 * C]

    def convolve(w, im, out):
        for j in range(0, SLABS, 2):
            lanes = pl.ds(j * PLANE, 2 * PLANE)
            out[:, lanes] = dot(w[...], im[:, lanes])

    def summed(y, x, centre, v):
        return (
            dot(centre[...], v[x * C : (x + 3) * C, 0:PLANE])
            + y[0:C, x * PLANE : (x + 1) * PLANE]
            + y[C : 2 * C, (x + 1) * PLANE : (x + 2) * PLANE]
            + y[2 * C : 3 * C, (x + 2) * PLANE : (x + 3) * PLANE]
        )

    def arrive(slot):
        for copy in sent[slot]:
            copy.wait_recv()

    def chunk(index):
        return pl.ds(pl.multiple_of(index * 16, 16), 16)

    def scatter_copy(o):
        t = lax.rem(rank + o, group)
        return pltpu.make_async_remote_copy(
            src_ref=g_send.at[chunk(t), :],
            dst_ref=g_slots.at[o],
            send_sem=s1_send.at[0],
            recv_sem=s1_recv.at[0],
            device_id=at(ring * group + t),
            device_id_type=MESH,
        )

    def ring_copy(o):
        t = lax.rem(ring + o, rings)
        return pltpu.make_async_remote_copy(
            src_ref=z_slots.at[ring],
            dst_ref=z_slots.at[ring],
            send_sem=s2_send.at[0],
            recv_sem=s2_recv.at[0],
            device_id=at(t * group + rank),
            device_id_type=MESH,
        )

    def gather_copy(o):
        t = lax.rem(rank + o, group)
        return pltpu.make_async_remote_copy(
            src_ref=r_send,
            dst_ref=fin.at[chunk(rank), :],
            send_sem=s3_send.at[0],
            recv_sem=s3_recv.at[0],
            device_id=at(ring * group + t),
            device_id_type=MESH,
        )

    def all_of(slots, send_sem, recv_sem):
        return pltpu.make_async_remote_copy(
            src_ref=slots,
            dst_ref=slots,
            send_sem=send_sem.at[0],
            recv_sem=recv_sem.at[0],
            device_id=at(nxt),
            device_id_type=MESH,
        )

    scattered = all_of(g_slots.at[pl.ds(1, group - 1)], s1_send, s1_recv)
    ringed = all_of(z_slots.at[pl.ds(1, rings - 1)], s2_send, s2_recv)
    gathered = all_of(g_slots.at[pl.ds(1, group - 1)], s3_send, s3_recv)

    arrive(0)
    take_rims(v_f, im_f, 0)
    convolve(w_one, im_f, y_buf)
    for x in range(EDGE):
        pre = summed(y_buf, x, c_one, v_f)
        pre_buf[x * C : (x + 1) * C, :] = pre
        value = (jax.nn.silu(pre) * keep_buf[x * C : (x + 1) * C, :]).astype(BF)
        v_d[(x + 1) * C : (x + 2) * C, 0:PLANE] = value
        for k in range(3):
            d_all[k * C : (k + 1) * C, (x + k) * PLANE : (x + k + 1) * PLANE] = value
    pack_faces(v_d, 2)
    sent.append(send_faces(2))

    arrive(1)
    take_rims(v_u, im_u, 1)

    g_two = dot_nt(d_all[...], im_u[...])
    g_full[0:256, :] = jnp.transpose(jnp.concatenate([g_two, jnp.zeros((C, 256), F32)], axis=0))
    centre = dot_nt(v_u[0:C, 0:PLANE], d_all[:, 0:PLANE])
    for j in range(1, SLABS):
        centre = centre + dot_nt(
            v_u[j * C : (j + 1) * C, 0:PLANE], d_all[:, j * PLANE : (j + 1) * PLANE]
        )
    g_full[256:288, :] = jnp.concatenate([centre, jnp.zeros((C, C), F32)], axis=1)
    g_send[0:288, :] = g_full[0:288, :].astype(BF)

    convolve(wt_two, im_u, z_buf)
    for x in range(EDGE):
        pre = pre_buf[x * C : (x + 1) * C, :]
        back = summed(z_buf, x, ct_two, v_u)
        logistic = jax.nn.sigmoid(pre)
        keep = keep_buf[x * C : (x + 1) * C, :]
        value = (back * keep * logistic * (1.0 + pre * (1.0 - logistic))).astype(BF)
        v_i[(x + 1) * C : (x + 2) * C, 0:PLANE] = value
        for k in range(3):
            i_all[k * C : (k + 1) * C, (x + k) * PLANE : (x + k + 1) * PLANE] = value

    g_one = dot_nt(i_all[...], im_f[...])
    g_full[288:384, :] = g_one[:, 0:128]
    g_full[384:480, :] = g_one[:, 128:256]
    centre = dot_nt(v_i[C : 2 * C, 0:PLANE], v_f[0 : 3 * C, 0:PLANE])
    for x in range(1, EDGE):
        centre = centre + dot_nt(
            v_i[(x + 1) * C : (x + 2) * C, 0:PLANE], v_f[x * C : (x + 3) * C, 0:PLANE]
        )
    g_full[480:512, :] = jnp.concatenate([centre, jnp.zeros((C, C), F32)], axis=1)
    g_send[288:512, :] = g_full[288:512, :].astype(BF)
    for o in range(1, group):
        scatter_copy(o).start()
    pack_faces(v_i, 3)
    sent.append(send_faces(3))

    shift_here(v_d, im_d)
    shift_here(v_i, im_i)

    scattered.wait_recv()
    total = g_full[chunk(rank), :]
    for o in range(1, group):
        total = total + g_slots[o].astype(F32)
    z_slots[ring] = total
    for o in range(1, rings):
        ring_copy(o).start()

    arrive(2)
    take_rims(v_d, im_d, 2)
    convolve(w_two, im_d, y_buf)
    for x in range(EDGE):
        enc_ref[0, :, x * PLANE : (x + 1) * PLANE] = summed(y_buf, x, c_two, v_d).astype(BF)
    out_enc = pltpu.make_async_copy(enc_ref, enc_hbm, out_sem.at[0])
    out_enc.start()

    ringed.wait_recv()
    total = z_slots[0]
    for o in range(1, rings):
        total = total + z_slots[o]
    r_send[...] = total.astype(BF)
    fin[chunk(rank), :] = total.astype(BF)
    for o in range(1, group):
        gather_copy(o).start()

    arrive(3)
    take_rims(v_i, im_i, 3)
    convolve(wt_one, im_i, z_buf)
    for x in range(EDGE):
        gfeat_ref[0, :, x * PLANE : (x + 1) * PLANE] = summed(z_buf, x, ct_one, v_i).astype(BF)
    out_gfeat = pltpu.make_async_copy(gfeat_ref, gfeat_hbm, out_sem.at[1])
    out_gfeat.start()

    gathered.wait_recv()
    out_fin = pltpu.make_async_copy(fin, fin_hbm, out_sem.at[2])
    out_fin.start()

    for pair in sent:
        for copy in pair:
            copy.wait_send()
    scattered.wait_send()
    ringed.wait_send()
    gathered.wait_send()
    for copy in (out_enc, out_gfeat, out_fin):
        copy.wait()


def write_out(
    count,
    enc_hbm,
    gfeat_hbm,
    fin_hbm,
    enc_out,
    gfeat_out,
    one_out,
    two_out,
    enc_buf,
    gfeat_buf,
    fin,
    one_buf,
    two_buf,
    sem,
):
    load_fin = pltpu.make_async_copy(fin_hbm, fin, sem.at[0])
    load_enc = pltpu.make_async_copy(enc_hbm, enc_buf, sem.at[1])
    load_gfeat = pltpu.make_async_copy(gfeat_hbm, gfeat_buf, sem.at[2])
    for copy in (load_fin, load_enc, load_gfeat):
        copy.start()
    stores = [
        pltpu.make_async_copy(one_buf, one_out, sem.at[3]),
        pltpu.make_async_copy(two_buf, two_out, sem.at[4]),
        pltpu.make_async_copy(enc_buf, enc_out, sem.at[5]),
        pltpu.make_async_copy(gfeat_buf, gfeat_out, sem.at[6]),
    ]
    load_fin.wait()
    norm = F32(1.0 / math.sqrt(count * EDGE**3))
    for k in range(3):
        for s in range(9):
            p, q = PLACE[s], PLACE[8 - s]
            if p < 8:
                top, left = 288 + 96 * (p // 4) + k * C, (p % 4) * C
            else:
                top, left = 480, k * C
            rows = fin[top : top + C, :].astype(F32)
            one_buf[k * 9 + s] = rows[:, left : left + C] * norm
            rows = fin[q * C : (q + 1) * C, :].astype(F32)
            two_buf[k * 9 + s] = rows[:, (2 - k) * C : (3 - k) * C] * norm
    stores[0].start()
    stores[1].start()
    load_enc.wait()
    stores[2].start()
    load_gfeat.wait()
    stores[3].start()
    for copy in stores:
        copy.wait()


def local(count, *args):
    features, pool, skip, one, two, links, positions, seed = args
    shift = jnp.asarray(shift_matrices(), BF)
    face = jnp.asarray(face_matrix(), BF)
    rows, lanes = SLABS * C, SLABS * PLANE
    dma = pltpu.SemaphoreType.DMA
    rings = count // 32
    hbm = pl.BlockSpec(memory_space=pltpu.HBM)
    field = jax.ShapeDtypeStruct((1, C, EDGE**3), BF)
    weight = jax.ShapeDtypeStruct((27, C, C), F32)
    done = pl.pallas_call(
        functools.partial(kernel, count),
        out_shape=(field, field, jax.ShapeDtypeStruct((512, 128), BF)),
        in_specs=[hbm] * 10,
        out_specs=(hbm,) * 3,
        scratch_shapes=[pltpu.VMEM((1, C, EDGE**3), BF)] * 5
        + [pltpu.VMEM((27, C, C), BF)] * 2
        + [pltpu.VMEM((PLANE + 128, 8 * PLANE), BF), pltpu.VMEM((2 * PLANE, 128), BF)]
        + [
            pltpu.SMEM((1, 6), jnp.int32),
            pltpu.SMEM((1, 3), jnp.int32),
            pltpu.SMEM((1,), jnp.int32),
        ]
        + [pltpu.VMEM((rows, PLANE + 128), BF)] * 4
        + [pltpu.VMEM((8 * C, lanes), BF)] * 4
        + [pltpu.VMEM((96, 256), BF)] * 4
        + [pltpu.VMEM((C, 96), BF)] * 4
        + [pltpu.VMEM((96, lanes), F32)] * 2
        + [pltpu.VMEM((EDGE * C, PLANE), F32)] * 2
        + [pltpu.VMEM((96, lanes), BF)] * 2
        + [pltpu.VMEM((4, 384, 128), BF)] * 3
        + [
            pltpu.VMEM((512, 128), F32),
            pltpu.VMEM((512, 128), BF),
            pltpu.VMEM((32, 16, 128), BF),
            pltpu.VMEM((rings, 16, 128), F32),
            pltpu.VMEM((16, 128), BF),
            pltpu.VMEM((512, 128), BF),
            dma((10,)),
            dma((3,)),
            dma((8,)),
            dma((8,)),
            dma((1,)),
            dma((1,)),
            dma((1,)),
            dma((1,)),
            dma((1,)),
            dma((1,)),
        ],
        compiler_params=pltpu.CompilerParams(
            collective_id=0, has_side_effects=True, vmem_limit_bytes=64 * 2**20
        ),
        cost_estimate=pl.CostEstimate(
            flops=4_000_000_000, bytes_accessed=3_000_000, transcendentals=300_000
        ),
    )(features, pool, skip, one, two, shift, face, links, positions, seed)
    return pl.pallas_call(
        functools.partial(write_out, count),
        out_shape=(field, field, weight, weight),
        in_specs=[hbm] * 3,
        out_specs=(hbm,) * 4,
        scratch_shapes=[pltpu.VMEM((1, C, EDGE**3), BF)] * 2
        + [pltpu.VMEM((512, 128), BF)]
        + [pltpu.VMEM((27, C, C), F32)] * 2
        + [dma((7,))],
        compiler_params=pltpu.CompilerParams(vmem_limit_bytes=64 * 2**20),
        cost_estimate=pl.CostEstimate(flops=0, bytes_accessed=2_000_000, transcendentals=0),
    )(*done)


def solution(mesh):
    both = ("blocks", "section")
    in_specs = (
        P(both, None, None),
        P(both, None, None),
        P(both, None, None),
        P(),
        P(),
        P(both, None),
        P(both, None),
        P(),
    )
    out_specs = (P(both, None, None), P(both, None, None), P(), P())
    return jax.shard_map(
        functools.partial(local, mesh.size),
        mesh=mesh,
        in_specs=in_specs,
        out_specs=out_specs,
        check_vma=False,
    )
```

```python
import functools
import math

import jax
import jax.numpy as jnp
import numpy as np
from jax import lax
from jax.experimental import pallas as pl
from jax.experimental.pallas import tpu as pltpu
from jax.sharding import PartitionSpec as P

C = 32
EDGE = 16
PLANE = EDGE * EDGE
SLABS = EDGE + 2
KEEP = 1024.0 / 819.0
MESH = pl.DeviceIdType.MESH
BF = jnp.bfloat16
F32 = jnp.float32

SHIFTS = [s for s in range(9) if s != 4] + [4]
PLACE = {s: i for i, s in enumerate(SHIFTS)}


def shift_matrices():
    table = np.zeros((PLANE + 128, 8 * PLANE), np.float32)
    for i, s in enumerate(SHIFTS[:8]):
        dy, dz = s // 3 - 1, s % 3 - 1
        for y in range(EDGE):
            for z in range(EDGE):
                column = i * PLANE + y * EDGE + z
                sy, sz = y + dy, z + dz
                in_y, in_z = 0 <= sy < EDGE, 0 <= sz < EDGE
                if in_y and in_z:
                    table[sy * EDGE + sz, column] = 1
                elif in_z:
                    slot = 0 if sy < 0 else 1
                    for half in (0, 64):
                        table[PLANE + half + slot * EDGE + sz, column] = 1
                elif in_y:
                    slot = 2 if sz < 0 else 3
                    for half in (0, 64):
                        table[PLANE + half + slot * EDGE + sy, column] = 1
    return table


def face_matrix():
    table = np.zeros((2 * PLANE, 128), np.float32)
    for half in (0, 1):
        for i in range(EDGE):
            base = half * 64
            table[half * PLANE + (EDGE - 1) * EDGE + i, base + i] = 1
            table[half * PLANE + i, base + EDGE + i] = 1
            table[half * PLANE + i * EDGE + EDGE - 1, base + 2 * EDGE + i] = 1
            table[half * PLANE + i * EDGE, base + 3 * EDGE + i] = 1
    return table


def far_first():
    steps = [(x, c, y) for x in range(4) for c in range(2) for y in range(4)][1:]
    return sorted(steps, key=lambda s: -(min(s[0], 4 - s[0]) + min(s[2], 4 - s[2]) + 0.1 * s[1]))


STEPS = far_first()
RING_STEPS = (4, 3, 5, 2, 6, 1, 7)


def dot(a, b):
    return jnp.dot(a, b, preferred_element_type=F32)


def dot_nt(a, b):
    return lax.dot_general(a, b, (((1,), (1,)), ((), ())), preferred_element_type=F32)


def kernel(
    count,
    feat_hbm,
    pool_hbm,
    skip_hbm,
    one_hbm,
    two_hbm,
    shift_hbm,
    face_hbm,
    links_hbm,
    pos_hbm,
    seed_hbm,
    enc_hbm,
    gfeat_hbm,
    fin_hbm,
    enc_ref,
    gfeat_ref,
    feat_ref,
    pool_ref,
    skip_ref,
    one_ref,
    two_ref,
    shift_ref,
    face_ref,
    links_ref,
    pos_ref,
    seed_ref,
    v_f,
    v_u,
    v_d,
    v_i,
    im_f,
    im_u,
    im_d,
    im_i,
    w_one,
    w_two,
    wt_one,
    wt_two,
    c_one,
    c_two,
    ct_one,
    ct_two,
    y_buf,
    z_buf,
    keep_buf,
    pre_buf,
    d_all,
    i_all,
    sendf,
    recvp,
    recvn,
    g_full,
    g_send,
    g_slots,
    z_slots,
    r_send,
    fin,
    in_sem,
    out_sem,
    fsend_sem,
    frecv_sem,
    s1_send,
    s1_recv,
    s2_send,
    s2_recv,
    s3_send,
    s3_recv,
):
    blocks, section = lax.axis_index("blocks"), lax.axis_index("section")
    per = lax.axis_size("section")
    me = blocks * per + section
    group = 32
    rings = count // group
    ring, rank = me // group, lax.rem(me, group)

    plane_x, core, plane_y = rank // 8, lax.rem(rank // 4, 2), lax.rem(rank, 4)

    def member(o):
        dx, dc, dy = STEPS[o - 1]
        return (
            lax.rem(plane_x + dx, 4) * 8 + lax.rem(core + dc, 2) * 4 + lax.rem(plane_y + dy, 4)
        )

    def at(index):
        return (index // per, lax.rem(index, per))

    nxt = lax.rem(me + 1, count)
    prv = lax.rem(me + count - 1, count)

    loads = {}
    for i, (name, src, dst) in enumerate(
        [
            ("feat", feat_hbm, feat_ref),
            ("face", face_hbm, face_ref),
            ("pool", pool_hbm, pool_ref),
            ("skip", skip_hbm, skip_ref),
            ("shift", shift_hbm, shift_ref),
            ("one", one_hbm, one_ref),
            ("two", two_hbm, two_ref),
            ("links", links_hbm, links_ref),
            ("pos", pos_hbm, pos_ref),
            ("seed", seed_hbm, seed_ref),
        ]
    ):
        loads[name] = pltpu.make_async_copy(src, dst, in_sem.at[i])
        loads[name].start()

    barrier = pltpu.get_barrier_semaphore()
    for d in (prv, nxt):
        pl.semaphore_signal(barrier, inc=1, device_id=at(d), device_id_type=MESH)

    for o in range(1, group):
        t = ring * group + member(o)
        pl.semaphore_signal(barrier, inc=1, device_id=at(t), device_id_type=MESH)
    for o in RING_STEPS:
        t = lax.rem(ring + o, rings) * group + rank
        pl.semaphore_signal(barrier, inc=1, device_id=at(t), device_id_type=MESH)

    loads["feat"].wait()
    for x in range(EDGE):
        rows, lanes = pl.ds((x + 1) * C, C), pl.ds(x * PLANE, PLANE)
        v_f[rows, 0:PLANE] = feat_ref[0, :, lanes]
    zero = jnp.zeros((C, 128), BF)
    for v in (v_f, v_u, v_d, v_i):
        v[0:C, PLANE:] = zero
        v[(SLABS - 1) * C :, PLANE:] = zero

    inner_rows = pl.ds(C, EDGE * C)

    def pack_faces(v, slot):
        last = EDGE * C
        sendf[slot, 0:32, :] = v[last : last + C, 0:128]
        sendf[slot, 32:64, :] = v[last : last + C, 128:256]
        sendf[slot, 64:96, :] = v[C : 2 * C, 0:128]
        sendf[slot, 96:128, :] = v[C : 2 * C, 128:256]
        packed = dot(v[C : 9 * C, 0:PLANE], face_ref[0:PLANE, :]) + dot(
            v[9 * C : 17 * C, 0:PLANE], face_ref[PLANE:, :]
        )
        sendf[slot, 128:384, :] = packed.astype(BF)

    def face_copies(slot):
        to_next = pltpu.make_async_remote_copy(
            src_ref=sendf.at[slot],
            dst_ref=recvp.at[slot],
            send_sem=fsend_sem.at[2 * slot],
            recv_sem=frecv_sem.at[2 * slot],
            device_id=at(nxt),
            device_id_type=MESH,
        )
        to_prev = pltpu.make_async_remote_copy(
            src_ref=sendf.at[slot],
            dst_ref=recvn.at[slot],
            send_sem=fsend_sem.at[2 * slot + 1],
            recv_sem=frecv_sem.at[2 * slot + 1],
            device_id=at(prv),
            device_id_type=MESH,
        )
        return to_next, to_prev

    def send_faces(slot):
        copies = face_copies(slot)
        for copy in copies:
            copy.start()
        return copies

    loads["face"].wait()
    pack_faces(v_f, 0)
    pl.semaphore_wait(barrier, 2 + (group - 1) + (rings - 1))
    sent = [send_faces(0)]

    loads["pool"].wait()
    loads["skip"].wait()
    for x in range(EDGE):
        rows, lanes = pl.ds((x + 1) * C, C), pl.ds(x * PLANE, PLANE)
        v_u[rows, 0:PLANE] = (
            pool_ref[0, :, lanes].astype(F32) + skip_ref[0, :, lanes].astype(F32)
        ).astype(BF)
    pack_faces(v_u, 1)
    sent.append(send_faces(1))

    for name in ("one", "two", "links", "pos", "seed", "shift"):
        loads[name].wait()

    def weights(ref, plain, mirrored, centre, mirrored_centre):
        for k in range(3):
            plain[k * C : (k + 1) * C, :] = jnp.concatenate(
                [ref[k * 9 + s].astype(F32) for s in SHIFTS[:8]], axis=1
            ).astype(BF)
        centre[...] = jnp.concatenate(
            [ref[k * 9 + 4].astype(F32) for k in range(3)], axis=1
        ).astype(BF)
        stacked = jnp.concatenate(
            [
                jnp.concatenate(
                    [ref[26 - (k * 9 + s)].astype(F32) for k in range(3)]
                    + [jnp.zeros((C, C), F32)],
                    axis=1,
                )
                for s in SHIFTS
            ]
            + [jnp.zeros((96, 128), F32)],
            axis=0,
        )
        turned = jnp.transpose(stacked)
        mirrored[...] = turned[0:96, 0:256].astype(BF)
        mirrored_centre[...] = jnp.concatenate(
            [turned[k * C : (k + 1) * C, 256:288] for k in range(3)], axis=1
        ).astype(BF)

    weights(one_ref, w_one, wt_one, c_one, ct_one)
    weights(two_ref, w_two, wt_two, c_two, ct_two)

    lane = lax.broadcasted_iota(jnp.int32, (C, PLANE), 1)
    channel = lax.broadcasted_iota(jnp.int32, (C, PLANE), 0)
    base = (pos_ref[0, 1] * EDGE + lax.shift_right_logical(lane, 4)) * jnp.int32(19349663)
    base = base ^ ((pos_ref[0, 2] * EDGE + (lane & 15)) * jnp.int32(83492791))
    base = base ^ (channel * jnp.int32(1103515245))
    base = base ^ (seed_ref[0] * jnp.int32(668265263))
    for x in range(EDGE):
        h = base ^ ((pos_ref[0, 0] * EDGE + x) * jnp.int32(73856093))
        h = h ^ lax.shift_right_logical(h, 13)
        h = h * jnp.int32(1274126177)
        h = h ^ lax.shift_right_logical(h, 16)
        keep_buf[x * C : (x + 1) * C, :] = jnp.where((h & 1023) >= 205, F32(KEEP), F32(0.0))

    for k in range(3):
        for j in range(SLABS):
            if not 0 <= j - k < EDGE:
                for ref in (d_all, i_all):
                    ref[k * C : (k + 1) * C, j * PLANE : (j + 1) * PLANE] = jnp.zeros(
                        (C, PLANE), BF
                    )

    def shift_here(v, im):
        for i in range(8):
            moved = dot(v[inner_rows, 0:PLANE], shift_ref[0:PLANE, i * PLANE : (i + 1) * PLANE])
            for x in range(EDGE):
                im[i * C : (i + 1) * C, (x + 1) * PLANE : (x + 2) * PLANE] = moved[
                    x * C : (x + 1) * C
                ].astype(BF)

    shift_here(v_f, im_f)
    shift_here(v_u, im_u)
    for v, im in ((v_f, im_f), (v_u, im_u)):
        for j in range(1, SLABS - 1):
            im[8 * C :, j * PLANE : (j + 1) * PLANE] = v[j * C : (j + 1) * C, 0:PLANE]

    mlane = lax.broadcasted_iota(jnp.int32, (16, 128), 1)
    slot_of = lax.shift_right_logical(mlane, 4) & 3
    wanted = jnp.full((16, 128), -1, jnp.int32)
    for k in range(4):
        wanted = jnp.where(slot_of == k, links_ref[0, 2 + k], wanted)

    def weight_of(condition):
        return jnp.where(condition, F32(1.0), F32(0.0)).astype(BF)[0:1, :]

    low = mlane < 64
    p_low = weight_of((wanted == prv) & low)
    n_low = weight_of((wanted == nxt) & low)
    p_high = weight_of((wanted == prv) & (mlane >= 64))
    n_high = weight_of((wanted == nxt) & (mlane >= 64))
    x_masks = []
    for k in range(2):
        link = jnp.full((16, 128), links_ref[0, k], jnp.int32)
        x_masks.append((weight_of(link == prv), weight_of(link == nxt)))

    def take_rims(v, im, slot):
        for k in range(2):
            mp, mn = x_masks[k]
            row = 0 if k == 0 else (SLABS - 1) * C
            for half in range(2):
                at_rows = pl.ds(k * 64 + half * 32, 32)
                v[row : row + C, half * 128 : half * 128 + 128] = (
                    recvp[slot, at_rows, :] * mp + recvn[slot, at_rows, :] * mn
                )
        from_p, from_n = recvp[slot, 128:384, :], recvn[slot, 128:384, :]
        v[C : 9 * C, PLANE:] = from_p * p_low + from_n * n_low
        v[9 * C : 17 * C, PLANE:] = from_p * p_high + from_n * n_high
        if im.shape[0] > 8 * C:
            for j in (0, SLABS - 1):
                im[8 * C :, j * PLANE : (j + 1) * PLANE] = v[j * C : (j + 1) * C, 0:PLANE]
        outer = jnp.concatenate([v[0:C, 0:PLANE], v[(SLABS - 1) * C :, 0:PLANE]], axis=0)
        for i in range(8):
            rim = dot(v[inner_rows, PLANE:], shift_ref[PLANE:, i * PLANE : (i + 1) * PLANE])
            for x in range(EDGE):
                rows, lanes = pl.ds(i * C, C), pl.ds((x + 1) * PLANE, PLANE)
                im[rows, lanes] = im[rows, lanes] + rim[x * C : (x + 1) * C].astype(BF)
            ends = dot(outer, shift_ref[0:PLANE, i * PLANE : (i + 1) * PLANE]).astype(BF)
            im[i * C : (i + 1) * C, 0:PLANE] = ends[0:C]
            im[i * C : (i + 1) * C, (SLABS - 1) * PLANE :] = ends[C : 2 * C]

    def convolve(w, im, out):
        for j in range(0, SLABS, 2):
            lanes = pl.ds(j * PLANE, 2 * PLANE)
            out[:, lanes] = dot(w[...], im[0 : 8 * C, lanes])

    def summed(y, x, centre, v):
        return (
            dot(centre[...], v[x * C : (x + 3) * C, 0:PLANE])
            + y[0:C, x * PLANE : (x + 1) * PLANE]
            + y[C : 2 * C, (x + 1) * PLANE : (x + 2) * PLANE]
            + y[2 * C : 3 * C, (x + 2) * PLANE : (x + 3) * PLANE]
        )

    def arrive(slot):
        for copy in sent[slot]:
            copy.wait_recv()

    def chunk(index):
        return pl.ds(pl.multiple_of(index * 16, 16), 16)

    def scatter_copy(o):
        t = member(o)
        return pltpu.make_async_remote_copy(
            src_ref=g_send.at[chunk(t), :],
            dst_ref=g_slots.at[o],
            send_sem=s1_send.at[0],
            recv_sem=s1_recv.at[0],
            device_id=at(ring * group + t),
            device_id_type=MESH,
        )

    def ring_copy(o):
        t = lax.rem(ring + o, rings)
        return pltpu.make_async_remote_copy(
            src_ref=z_slots.at[ring],
            dst_ref=z_slots.at[ring],
            send_sem=s2_send.at[0],
            recv_sem=s2_recv.at[0],
            device_id=at(t * group + rank),
            device_id_type=MESH,
        )

    def gather_copy(o):
        t = member(o)
        return pltpu.make_async_remote_copy(
            src_ref=r_send,
            dst_ref=fin.at[chunk(rank), :],
            send_sem=s3_send.at[0],
            recv_sem=s3_recv.at[0],
            device_id=at(ring * group + t),
            device_id_type=MESH,
        )

    def all_of(slots, send_sem, recv_sem):
        return pltpu.make_async_remote_copy(
            src_ref=slots,
            dst_ref=slots,
            send_sem=send_sem.at[0],
            recv_sem=recv_sem.at[0],
            device_id=at(nxt),
            device_id_type=MESH,
        )

    scattered = all_of(g_slots.at[pl.ds(1, group - 1)], s1_send, s1_recv)
    ringed = all_of(z_slots.at[pl.ds(1, rings - 1)], s2_send, s2_recv)
    gathered = all_of(g_slots.at[pl.ds(1, group - 1)], s3_send, s3_recv)

    arrive(0)
    take_rims(v_f, im_f, 0)
    convolve(w_one, im_f, y_buf)
    for x in range(EDGE):
        pre = summed(y_buf, x, c_one, v_f)
        pre_buf[x * C : (x + 1) * C, :] = pre
        value = (jax.nn.silu(pre) * keep_buf[x * C : (x + 1) * C, :]).astype(BF)
        v_d[(x + 1) * C : (x + 2) * C, 0:PLANE] = value
        for k in range(3):
            d_all[k * C : (k + 1) * C, (x + k) * PLANE : (x + k + 1) * PLANE] = value
    pack_faces(v_d, 2)
    sent.append(send_faces(2))
    for x in range(EDGE):
        pre = pre_buf[x * C : (x + 1) * C, :]
        logistic = jax.nn.sigmoid(pre)
        keep = keep_buf[x * C : (x + 1) * C, :]
        pre_buf[x * C : (x + 1) * C, :] = keep * logistic * (1.0 + pre * (1.0 - logistic))

    arrive(1)
    take_rims(v_u, im_u, 1)

    g_two = dot_nt(im_u[...], d_all[...])
    g_full[0:288, :] = jnp.concatenate([g_two, jnp.zeros((9 * C, C), F32)], axis=1)
    g_send[0:288, :] = g_full[0:288, :].astype(BF)

    convolve(wt_two, im_u, z_buf)
    for x in range(EDGE):
        back = summed(z_buf, x, ct_two, v_u)
        value = (back * pre_buf[x * C : (x + 1) * C, :]).astype(BF)
        v_i[(x + 1) * C : (x + 2) * C, 0:PLANE] = value
        for k in range(3):
            i_all[k * C : (k + 1) * C, (x + k) * PLANE : (x + k + 1) * PLANE] = value

    g_one = dot_nt(i_all[...], im_f[...])
    g_full[288:384, :] = g_one[:, 0:128]
    g_full[384:480, :] = g_one[:, 128:256]
    g_full[480:512, :] = jnp.concatenate(
        [g_one[k * C : (k + 1) * C, 256:288] for k in range(3)] + [jnp.zeros((C, C), F32)], axis=1
    )
    g_send[288:512, :] = g_full[288:512, :].astype(BF)
    for o in range(1, group):
        scatter_copy(o).start()
    pack_faces(v_i, 3)
    sent.append(send_faces(3))

    shift_here(v_d, im_d)
    shift_here(v_i, im_i)

    scattered.wait_recv()
    total = g_full[chunk(rank), :]
    for o in range(1, group):
        total = total + g_slots[o].astype(F32)
    z_slots[ring] = total
    for o in RING_STEPS:
        ring_copy(o).start()

    arrive(2)
    take_rims(v_d, im_d, 2)
    convolve(w_two, im_d, y_buf)
    for x in range(EDGE):
        enc_ref[0, :, x * PLANE : (x + 1) * PLANE] = summed(y_buf, x, c_two, v_d).astype(BF)
    out_enc = pltpu.make_async_copy(enc_ref, enc_hbm, out_sem.at[0])
    out_enc.start()

    ringed.wait_recv()
    total = z_slots[0]
    for o in range(1, rings):
        total = total + z_slots[o]
    r_send[...] = total.astype(BF)
    fin[chunk(rank), :] = total.astype(BF)
    for o in range(1, group):
        gather_copy(o).start()

    arrive(3)
    take_rims(v_i, im_i, 3)
    convolve(wt_one, im_i, z_buf)
    for x in range(EDGE):
        gfeat_ref[0, :, x * PLANE : (x + 1) * PLANE] = summed(z_buf, x, ct_one, v_i).astype(BF)
    out_gfeat = pltpu.make_async_copy(gfeat_ref, gfeat_hbm, out_sem.at[1])
    out_gfeat.start()

    gathered.wait_recv()
    out_fin = pltpu.make_async_copy(fin, fin_hbm, out_sem.at[2])
    out_fin.start()

    for pair in sent:
        for copy in pair:
            copy.wait_send()
    scattered.wait_send()
    ringed.wait_send()
    gathered.wait_send()
    for copy in (out_enc, out_gfeat, out_fin):
        copy.wait()


def write_out(
    count,
    enc_hbm,
    gfeat_hbm,
    fin_hbm,
    enc_out,
    gfeat_out,
    one_out,
    two_out,
    enc_buf,
    gfeat_buf,
    fin,
    one_buf,
    two_buf,
    sem,
):
    load_fin = pltpu.make_async_copy(fin_hbm, fin, sem.at[0])
    load_enc = pltpu.make_async_copy(enc_hbm, enc_buf, sem.at[1])
    load_gfeat = pltpu.make_async_copy(gfeat_hbm, gfeat_buf, sem.at[2])
    for copy in (load_fin, load_enc, load_gfeat):
        copy.start()
    stores = [
        pltpu.make_async_copy(one_buf, one_out, sem.at[3]),
        pltpu.make_async_copy(two_buf, two_out, sem.at[4]),
        pltpu.make_async_copy(enc_buf, enc_out, sem.at[5]),
        pltpu.make_async_copy(gfeat_buf, gfeat_out, sem.at[6]),
    ]
    load_fin.wait()
    norm = F32(1.0 / math.sqrt(count * EDGE**3))
    for k in range(3):
        for s in range(9):
            p, q = PLACE[s], PLACE[8 - s]
            if p < 8:
                top, left = 288 + 96 * (p // 4) + k * C, (p % 4) * C
            else:
                top, left = 480, k * C
            rows = fin[top : top + C, :].astype(F32)
            one_buf[k * 9 + s] = rows[:, left : left + C] * norm
            rows = fin[q * C : (q + 1) * C, :].astype(F32)
            two_buf[k * 9 + s] = rows[:, (2 - k) * C : (3 - k) * C] * norm
    stores[0].start()
    stores[1].start()
    load_enc.wait()
    stores[2].start()
    load_gfeat.wait()
    stores[3].start()
    for copy in stores:
        copy.wait()


def local(count, *args):
    features, pool, skip, one, two, links, positions, seed = args
    shift = jnp.asarray(shift_matrices(), BF)
    face = jnp.asarray(face_matrix(), BF)
    rows, lanes = SLABS * C, SLABS * PLANE
    dma = pltpu.SemaphoreType.DMA
    rings = count // 32
    hbm = pl.BlockSpec(memory_space=pltpu.HBM)
    field = jax.ShapeDtypeStruct((1, C, EDGE**3), BF)
    weight = jax.ShapeDtypeStruct((27, C, C), F32)
    done = pl.pallas_call(
        functools.partial(kernel, count),
        out_shape=(field, field, jax.ShapeDtypeStruct((512, 128), BF)),
        in_specs=[hbm] * 10,
        out_specs=(hbm,) * 3,
        scratch_shapes=[pltpu.VMEM((1, C, EDGE**3), BF)] * 5
        + [pltpu.VMEM((27, C, C), BF)] * 2
        + [pltpu.VMEM((PLANE + 128, 8 * PLANE), BF), pltpu.VMEM((2 * PLANE, 128), BF)]
        + [
            pltpu.SMEM((1, 6), jnp.int32),
            pltpu.SMEM((1, 3), jnp.int32),
            pltpu.SMEM((1,), jnp.int32),
        ]
        + [pltpu.VMEM((rows, PLANE + 128), BF)] * 4
        + [pltpu.VMEM((9 * C, lanes), BF)] * 2
        + [pltpu.VMEM((8 * C, lanes), BF)] * 2
        + [pltpu.VMEM((96, 256), BF)] * 4
        + [pltpu.VMEM((C, 96), BF)] * 4
        + [pltpu.VMEM((96, lanes), F32)] * 2
        + [pltpu.VMEM((EDGE * C, PLANE), F32)] * 2
        + [pltpu.VMEM((96, lanes), BF)] * 2
        + [pltpu.VMEM((4, 384, 128), BF)] * 3
        + [
            pltpu.VMEM((512, 128), F32),
            pltpu.VMEM((512, 128), BF),
            pltpu.VMEM((32, 16, 128), BF),
            pltpu.VMEM((rings, 16, 128), F32),
            pltpu.VMEM((16, 128), BF),
            pltpu.VMEM((512, 128), BF),
            dma((10,)),
            dma((3,)),
            dma((8,)),
            dma((8,)),
            dma((1,)),
            dma((1,)),
            dma((1,)),
            dma((1,)),
            dma((1,)),
            dma((1,)),
        ],
        compiler_params=pltpu.CompilerParams(
            collective_id=0, has_side_effects=True, vmem_limit_bytes=64 * 2**20
        ),
        cost_estimate=pl.CostEstimate(
            flops=4_000_000_000, bytes_accessed=3_000_000, transcendentals=300_000
        ),
    )(features, pool, skip, one, two, shift, face, links, positions, seed)
    return pl.pallas_call(
        functools.partial(write_out, count),
        out_shape=(field, field, weight, weight),
        in_specs=[hbm] * 3,
        out_specs=(hbm,) * 4,
        scratch_shapes=[pltpu.VMEM((1, C, EDGE**3), BF)] * 2
        + [pltpu.VMEM((512, 128), BF)]
        + [pltpu.VMEM((27, C, C), F32)] * 2
        + [dma((7,))],
        compiler_params=pltpu.CompilerParams(vmem_limit_bytes=64 * 2**20),
        cost_estimate=pl.CostEstimate(flops=0, bytes_accessed=2_000_000, transcendentals=0),
    )(*done)


def solution(mesh):
    both = ("blocks", "section")
    in_specs = (
        P(both, None, None),
        P(both, None, None),
        P(both, None, None),
        P(),
        P(),
        P(both, None),
        P(both, None),
        P(),
    )
    out_specs = (P(both, None, None), P(both, None, None), P(), P())
    return jax.shard_map(
        functools.partial(local, mesh.size),
        mesh=mesh,
        in_specs=in_specs,
        out_specs=out_specs,
        check_vma=False,
    )
```

```python
import functools
import math

import jax
import jax.numpy as jnp
import numpy as np
from jax import lax
from jax.experimental import pallas as pl
from jax.experimental.pallas import tpu as pltpu
from jax.sharding import PartitionSpec as P

C = 32
EDGE = 16
PLANE = EDGE * EDGE
SLABS = EDGE + 2
KEEP = 1024.0 / 819.0
MESH = pl.DeviceIdType.MESH
BF = jnp.bfloat16
F32 = jnp.float32

SHIFTS = [s for s in range(9) if s != 4] + [4]
PLACE = {s: i for i, s in enumerate(SHIFTS)}


def shift_matrices():
    table = np.zeros((PLANE + 128, 8 * PLANE), np.float32)
    for i, s in enumerate(SHIFTS[:8]):
        dy, dz = s // 3 - 1, s % 3 - 1
        for y in range(EDGE):
            for z in range(EDGE):
                column = i * PLANE + y * EDGE + z
                sy, sz = y + dy, z + dz
                in_y, in_z = 0 <= sy < EDGE, 0 <= sz < EDGE
                if in_y and in_z:
                    table[sy * EDGE + sz, column] = 1
                elif in_z:
                    slot = 0 if sy < 0 else 1
                    for half in (0, 64):
                        table[PLANE + half + slot * EDGE + sz, column] = 1
                elif in_y:
                    slot = 2 if sz < 0 else 3
                    for half in (0, 64):
                        table[PLANE + half + slot * EDGE + sy, column] = 1
    return table


def face_matrix():
    table = np.zeros((2 * PLANE, 128), np.float32)
    for half in (0, 1):
        for i in range(EDGE):
            base = half * 64
            table[half * PLANE + (EDGE - 1) * EDGE + i, base + i] = 1
            table[half * PLANE + i, base + EDGE + i] = 1
            table[half * PLANE + i * EDGE + EDGE - 1, base + 2 * EDGE + i] = 1
            table[half * PLANE + i * EDGE, base + 3 * EDGE + i] = 1
    return table


def far_first():
    steps = [(x, c, y) for x in range(4) for c in range(2) for y in range(4)][1:]
    return sorted(steps, key=lambda s: -(min(s[0], 4 - s[0]) + min(s[2], 4 - s[2]) + 0.1 * s[1]))


STEPS = far_first()
RING_STEPS = (4, 3, 5, 2, 6, 1, 7)


def dot(a, b):
    return jnp.dot(a, b, preferred_element_type=F32)


def dot_nt(a, b):
    return lax.dot_general(a, b, (((1,), (1,)), ((), ())), preferred_element_type=F32)


def kernel(
    count,
    feat_hbm,
    pool_hbm,
    skip_hbm,
    one_hbm,
    two_hbm,
    shift_hbm,
    face_hbm,
    links_hbm,
    pos_hbm,
    seed_hbm,
    enc_hbm,
    gfeat_hbm,
    fin_hbm,
    enc_ref,
    gfeat_ref,
    feat_ref,
    pool_ref,
    skip_ref,
    one_ref,
    two_ref,
    shift_ref,
    face_ref,
    links_ref,
    pos_ref,
    seed_ref,
    v_f,
    v_u,
    v_d,
    v_i,
    im_f,
    im_u,
    im_d,
    im_i,
    w_one,
    w_two,
    wt_one,
    wt_two,
    c_one,
    c_two,
    ct_one,
    ct_two,
    y_buf,
    z_buf,
    keep_buf,
    pre_buf,
    d_all,
    i_all,
    sendf,
    recvp,
    recvn,
    g_full,
    g_send,
    g_slots,
    z_slots,
    r_send,
    fin,
    know_sem,
    in_sem,
    out_sem,
    fsend_sem,
    frecv_sem,
    s1_send,
    s1_recv,
    s2_send,
    s2_recv,
    s3_send,
    s3_recv,
):
    blocks, section = lax.axis_index("blocks"), lax.axis_index("section")
    per = lax.axis_size("section")
    me = blocks * per + section
    group = 32
    rings = count // group
    ring, rank = me // group, lax.rem(me, group)

    plane_x, core, plane_y = rank // 8, lax.rem(rank // 4, 2), lax.rem(rank, 4)

    def member(o):
        dx, dc, dy = STEPS[o - 1]
        return (
            lax.rem(plane_x + dx, 4) * 8 + lax.rem(core + dc, 2) * 4 + lax.rem(plane_y + dy, 4)
        )

    def at(index):
        return (index // per, lax.rem(index, per))

    nxt = lax.rem(me + 1, count)
    prv = lax.rem(me + count - 1, count)

    loads = {}
    for i, (name, src, dst) in enumerate(
        [
            ("feat", feat_hbm, feat_ref),
            ("face", face_hbm, face_ref),
            ("pool", pool_hbm, pool_ref),
            ("skip", skip_hbm, skip_ref),
            ("shift", shift_hbm, shift_ref),
            ("one", one_hbm, one_ref),
            ("two", two_hbm, two_ref),
            ("links", links_hbm, links_ref),
            ("pos", pos_hbm, pos_ref),
            ("seed", seed_hbm, seed_ref),
        ]
    ):
        loads[name] = pltpu.make_async_copy(src, dst, in_sem.at[i])
        loads[name].start()

    barrier = pltpu.get_barrier_semaphore()
    for d in (prv, nxt):
        pl.semaphore_signal(barrier, inc=1, device_id=at(d), device_id_type=MESH)

    for o in range(1, group):
        t = ring * group + member(o)
        pl.semaphore_signal(barrier, inc=1, device_id=at(t), device_id_type=MESH)
    for o in (1, rings - 1):
        t = lax.rem(ring + o, rings) * group + rank
        pl.semaphore_signal(barrier, inc=1, device_id=at(t), device_id_type=MESH)

    loads["feat"].wait()
    for x in range(EDGE):
        rows, lanes = pl.ds((x + 1) * C, C), pl.ds(x * PLANE, PLANE)
        v_f[rows, 0:PLANE] = feat_ref[0, :, lanes]
    zero = jnp.zeros((C, 128), BF)
    for v in (v_f, v_u, v_d, v_i):
        v[0:C, PLANE:] = zero
        v[(SLABS - 1) * C :, PLANE:] = zero

    inner_rows = pl.ds(C, EDGE * C)

    def pack_faces(v, slot):
        last = EDGE * C
        sendf[slot, 0:32, :] = v[last : last + C, 0:128]
        sendf[slot, 32:64, :] = v[last : last + C, 128:256]
        sendf[slot, 64:96, :] = v[C : 2 * C, 0:128]
        sendf[slot, 96:128, :] = v[C : 2 * C, 128:256]
        packed = dot(v[C : 9 * C, 0:PLANE], face_ref[0:PLANE, :]) + dot(
            v[9 * C : 17 * C, 0:PLANE], face_ref[PLANE:, :]
        )
        sendf[slot, 128:384, :] = packed.astype(BF)

    def face_copies(slot):
        to_next = pltpu.make_async_remote_copy(
            src_ref=sendf.at[slot],
            dst_ref=recvp.at[slot],
            send_sem=fsend_sem.at[2 * slot],
            recv_sem=frecv_sem.at[2 * slot],
            device_id=at(nxt),
            device_id_type=MESH,
        )
        to_prev = pltpu.make_async_remote_copy(
            src_ref=sendf.at[slot],
            dst_ref=recvn.at[slot],
            send_sem=fsend_sem.at[2 * slot + 1],
            recv_sem=frecv_sem.at[2 * slot + 1],
            device_id=at(prv),
            device_id_type=MESH,
        )
        return to_next, to_prev

    def send_faces(slot):
        copies = face_copies(slot)
        for copy in copies:
            copy.start()
        return copies

    loads["face"].wait()
    pack_faces(v_f, 0)
    pl.semaphore_wait(barrier, 2 + (group - 1) + 2)
    sent = [send_faces(0)]

    def tell(step, index):
        for o in (step, rings - step):
            t = lax.rem(ring + o, rings) * group + rank
            pl.semaphore_signal(know_sem.at[index], inc=1, device_id=at(t), device_id_type=MESH)

    tell(1, 0)

    loads["pool"].wait()
    loads["skip"].wait()
    for x in range(EDGE):
        rows, lanes = pl.ds((x + 1) * C, C), pl.ds(x * PLANE, PLANE)
        v_u[rows, 0:PLANE] = (
            pool_ref[0, :, lanes].astype(F32) + skip_ref[0, :, lanes].astype(F32)
        ).astype(BF)
    pack_faces(v_u, 1)
    sent.append(send_faces(1))

    for name in ("one", "two", "links", "pos", "seed", "shift"):
        loads[name].wait()

    def weights(ref, plain, mirrored, centre, mirrored_centre):
        for k in range(3):
            plain[k * C : (k + 1) * C, :] = jnp.concatenate(
                [ref[k * 9 + s].astype(F32) for s in SHIFTS[:8]], axis=1
            ).astype(BF)
        centre[...] = jnp.concatenate(
            [ref[k * 9 + 4].astype(F32) for k in range(3)], axis=1
        ).astype(BF)
        stacked = jnp.concatenate(
            [
                jnp.concatenate(
                    [ref[26 - (k * 9 + s)].astype(F32) for k in range(3)]
                    + [jnp.zeros((C, C), F32)],
                    axis=1,
                )
                for s in SHIFTS
            ]
            + [jnp.zeros((96, 128), F32)],
            axis=0,
        )
        turned = jnp.transpose(stacked)
        mirrored[...] = turned[0:96, 0:256].astype(BF)
        mirrored_centre[...] = jnp.concatenate(
            [turned[k * C : (k + 1) * C, 256:288] for k in range(3)], axis=1
        ).astype(BF)

    weights(one_ref, w_one, wt_one, c_one, ct_one)
    weights(two_ref, w_two, wt_two, c_two, ct_two)

    lane = lax.broadcasted_iota(jnp.int32, (C, PLANE), 1)
    channel = lax.broadcasted_iota(jnp.int32, (C, PLANE), 0)
    base = (pos_ref[0, 1] * EDGE + lax.shift_right_logical(lane, 4)) * jnp.int32(19349663)
    base = base ^ ((pos_ref[0, 2] * EDGE + (lane & 15)) * jnp.int32(83492791))
    base = base ^ (channel * jnp.int32(1103515245))
    base = base ^ (seed_ref[0] * jnp.int32(668265263))
    for x in range(EDGE):
        h = base ^ ((pos_ref[0, 0] * EDGE + x) * jnp.int32(73856093))
        h = h ^ lax.shift_right_logical(h, 13)
        h = h * jnp.int32(1274126177)
        h = h ^ lax.shift_right_logical(h, 16)
        keep_buf[x * C : (x + 1) * C, :] = jnp.where((h & 1023) >= 205, F32(KEEP), F32(0.0))

    for k in range(3):
        for j in range(SLABS):
            if not 0 <= j - k < EDGE:
                for ref in (d_all, i_all):
                    ref[k * C : (k + 1) * C, j * PLANE : (j + 1) * PLANE] = jnp.zeros(
                        (C, PLANE), BF
                    )

    def shift_here(v, im):
        for i in range(8):
            moved = dot(v[inner_rows, 0:PLANE], shift_ref[0:PLANE, i * PLANE : (i + 1) * PLANE])
            for x in range(EDGE):
                im[i * C : (i + 1) * C, (x + 1) * PLANE : (x + 2) * PLANE] = moved[
                    x * C : (x + 1) * C
                ].astype(BF)

    shift_here(v_f, im_f)
    shift_here(v_u, im_u)
    for v, im in ((v_f, im_f), (v_u, im_u)):
        for j in range(1, SLABS - 1):
            im[8 * C :, j * PLANE : (j + 1) * PLANE] = v[j * C : (j + 1) * C, 0:PLANE]

    mlane = lax.broadcasted_iota(jnp.int32, (16, 128), 1)
    slot_of = lax.shift_right_logical(mlane, 4) & 3
    wanted = jnp.full((16, 128), -1, jnp.int32)
    for k in range(4):
        wanted = jnp.where(slot_of == k, links_ref[0, 2 + k], wanted)

    def weight_of(condition):
        return jnp.where(condition, F32(1.0), F32(0.0)).astype(BF)[0:1, :]

    low = mlane < 64
    p_low = weight_of((wanted == prv) & low)
    n_low = weight_of((wanted == nxt) & low)
    p_high = weight_of((wanted == prv) & (mlane >= 64))
    n_high = weight_of((wanted == nxt) & (mlane >= 64))
    x_masks = []
    for k in range(2):
        link = jnp.full((16, 128), links_ref[0, k], jnp.int32)
        x_masks.append((weight_of(link == prv), weight_of(link == nxt)))

    def take_rims(v, im, slot):
        for k in range(2):
            mp, mn = x_masks[k]
            row = 0 if k == 0 else (SLABS - 1) * C
            for half in range(2):
                at_rows = pl.ds(k * 64 + half * 32, 32)
                v[row : row + C, half * 128 : half * 128 + 128] = (
                    recvp[slot, at_rows, :] * mp + recvn[slot, at_rows, :] * mn
                )
        from_p, from_n = recvp[slot, 128:384, :], recvn[slot, 128:384, :]
        v[C : 9 * C, PLANE:] = from_p * p_low + from_n * n_low
        v[9 * C : 17 * C, PLANE:] = from_p * p_high + from_n * n_high
        if im.shape[0] > 8 * C:
            for j in (0, SLABS - 1):
                im[8 * C :, j * PLANE : (j + 1) * PLANE] = v[j * C : (j + 1) * C, 0:PLANE]
        outer = jnp.concatenate([v[0:C, 0:PLANE], v[(SLABS - 1) * C :, 0:PLANE]], axis=0)
        for i in range(8):
            rim = dot(v[inner_rows, PLANE:], shift_ref[PLANE:, i * PLANE : (i + 1) * PLANE])
            for x in range(EDGE):
                rows, lanes = pl.ds(i * C, C), pl.ds((x + 1) * PLANE, PLANE)
                im[rows, lanes] = im[rows, lanes] + rim[x * C : (x + 1) * C].astype(BF)
            ends = dot(outer, shift_ref[0:PLANE, i * PLANE : (i + 1) * PLANE]).astype(BF)
            im[i * C : (i + 1) * C, 0:PLANE] = ends[0:C]
            im[i * C : (i + 1) * C, (SLABS - 1) * PLANE :] = ends[C : 2 * C]

    def convolve(w, im, out):
        for j in range(0, SLABS, 2):
            lanes = pl.ds(j * PLANE, 2 * PLANE)
            out[:, lanes] = dot(w[...], im[0 : 8 * C, lanes])

    def summed(y, x, centre, v):
        return (
            dot(centre[...], v[x * C : (x + 3) * C, 0:PLANE])
            + y[0:C, x * PLANE : (x + 1) * PLANE]
            + y[C : 2 * C, (x + 1) * PLANE : (x + 2) * PLANE]
            + y[2 * C : 3 * C, (x + 2) * PLANE : (x + 3) * PLANE]
        )

    def arrive(slot):
        for copy in sent[slot]:
            copy.wait_recv()

    def chunk(index):
        return pl.ds(pl.multiple_of(index * 16, 16), 16)

    def scatter_copy(o):
        t = member(o)
        return pltpu.make_async_remote_copy(
            src_ref=g_send.at[chunk(t), :],
            dst_ref=g_slots.at[o],
            send_sem=s1_send.at[0],
            recv_sem=s1_recv.at[0],
            device_id=at(ring * group + t),
            device_id_type=MESH,
        )

    def ring_copy(o):
        t = lax.rem(ring + o, rings)
        return pltpu.make_async_remote_copy(
            src_ref=z_slots.at[ring],
            dst_ref=z_slots.at[ring],
            send_sem=s2_send.at[0],
            recv_sem=s2_recv.at[0],
            device_id=at(t * group + rank),
            device_id_type=MESH,
        )

    def gather_copy(o):
        t = member(o)
        return pltpu.make_async_remote_copy(
            src_ref=r_send,
            dst_ref=fin.at[chunk(rank), :],
            send_sem=s3_send.at[0],
            recv_sem=s3_recv.at[0],
            device_id=at(ring * group + t),
            device_id_type=MESH,
        )

    def all_of(slots, send_sem, recv_sem):
        return pltpu.make_async_remote_copy(
            src_ref=slots,
            dst_ref=slots,
            send_sem=send_sem.at[0],
            recv_sem=recv_sem.at[0],
            device_id=at(nxt),
            device_id_type=MESH,
        )

    scattered = all_of(g_slots.at[pl.ds(1, group - 1)], s1_send, s1_recv)
    ringed = all_of(z_slots.at[pl.ds(1, rings - 1)], s2_send, s2_recv)
    gathered = all_of(g_slots.at[pl.ds(1, group - 1)], s3_send, s3_recv)

    arrive(0)
    pl.semaphore_wait(know_sem.at[0], 2)
    tell(2, 1)
    take_rims(v_f, im_f, 0)
    convolve(w_one, im_f, y_buf)
    for x in range(EDGE):
        pre = summed(y_buf, x, c_one, v_f)
        pre_buf[x * C : (x + 1) * C, :] = pre
        value = (jax.nn.silu(pre) * keep_buf[x * C : (x + 1) * C, :]).astype(BF)
        v_d[(x + 1) * C : (x + 2) * C, 0:PLANE] = value
        for k in range(3):
            d_all[k * C : (k + 1) * C, (x + k) * PLANE : (x + k + 1) * PLANE] = value
    pack_faces(v_d, 2)
    sent.append(send_faces(2))
    for x in range(EDGE):
        pre = pre_buf[x * C : (x + 1) * C, :]
        logistic = jax.nn.sigmoid(pre)
        keep = keep_buf[x * C : (x + 1) * C, :]
        pre_buf[x * C : (x + 1) * C, :] = keep * logistic * (1.0 + pre * (1.0 - logistic))

    arrive(1)
    take_rims(v_u, im_u, 1)

    g_two = dot_nt(im_u[...], d_all[...])
    g_full[0:288, :] = jnp.concatenate([g_two, jnp.zeros((9 * C, C), F32)], axis=1)
    g_send[0:288, :] = g_full[0:288, :].astype(BF)

    convolve(wt_two, im_u, z_buf)
    for x in range(EDGE):
        back = summed(z_buf, x, ct_two, v_u)
        value = (back * pre_buf[x * C : (x + 1) * C, :]).astype(BF)
        v_i[(x + 1) * C : (x + 2) * C, 0:PLANE] = value
        for k in range(3):
            i_all[k * C : (k + 1) * C, (x + k) * PLANE : (x + k + 1) * PLANE] = value

    g_one = dot_nt(i_all[...], im_f[...])
    g_full[288:384, :] = g_one[:, 0:128]
    g_full[384:480, :] = g_one[:, 128:256]
    g_full[480:512, :] = jnp.concatenate(
        [g_one[k * C : (k + 1) * C, 256:288] for k in range(3)] + [jnp.zeros((C, C), F32)], axis=1
    )
    g_send[288:512, :] = g_full[288:512, :].astype(BF)
    for o in range(1, group):
        scatter_copy(o).start()
    pack_faces(v_i, 3)

    shift_here(v_d, im_d)
    shift_here(v_i, im_i)

    scattered.wait_recv()
    pl.semaphore_wait(know_sem.at[1], 2)
    total = g_full[chunk(rank), :]
    for o in range(1, group):
        total = total + g_slots[o].astype(F32)
    z_slots[ring] = total
    for o in RING_STEPS:
        ring_copy(o).start()
    sent.append(send_faces(3))

    arrive(2)
    take_rims(v_d, im_d, 2)
    convolve(w_two, im_d, y_buf)
    for x in range(EDGE):
        enc_ref[0, :, x * PLANE : (x + 1) * PLANE] = summed(y_buf, x, c_two, v_d).astype(BF)
    out_enc = pltpu.make_async_copy(enc_ref, enc_hbm, out_sem.at[0])
    out_enc.start()

    ringed.wait_recv()
    total = z_slots[0]
    for o in range(1, rings):
        total = total + z_slots[o]
    r_send[...] = total.astype(BF)
    fin[chunk(rank), :] = total.astype(BF)
    for o in range(1, group):
        gather_copy(o).start()

    arrive(3)
    take_rims(v_i, im_i, 3)
    convolve(wt_one, im_i, z_buf)
    for x in range(EDGE):
        gfeat_ref[0, :, x * PLANE : (x + 1) * PLANE] = summed(z_buf, x, ct_one, v_i).astype(BF)
    out_gfeat = pltpu.make_async_copy(gfeat_ref, gfeat_hbm, out_sem.at[1])
    out_gfeat.start()

    gathered.wait_recv()
    out_fin = pltpu.make_async_copy(fin, fin_hbm, out_sem.at[2])
    out_fin.start()

    for pair in sent:
        for copy in pair:
            copy.wait_send()
    scattered.wait_send()
    ringed.wait_send()
    gathered.wait_send()
    for copy in (out_enc, out_gfeat, out_fin):
        copy.wait()


def write_out(
    count,
    enc_hbm,
    gfeat_hbm,
    fin_hbm,
    enc_out,
    gfeat_out,
    one_out,
    two_out,
    enc_buf,
    gfeat_buf,
    fin,
    one_buf,
    two_buf,
    sem,
):
    load_fin = pltpu.make_async_copy(fin_hbm, fin, sem.at[0])
    load_enc = pltpu.make_async_copy(enc_hbm, enc_buf, sem.at[1])
    load_gfeat = pltpu.make_async_copy(gfeat_hbm, gfeat_buf, sem.at[2])
    for copy in (load_fin, load_enc, load_gfeat):
        copy.start()
    stores = [
        pltpu.make_async_copy(one_buf, one_out, sem.at[3]),
        pltpu.make_async_copy(two_buf, two_out, sem.at[4]),
        pltpu.make_async_copy(enc_buf, enc_out, sem.at[5]),
        pltpu.make_async_copy(gfeat_buf, gfeat_out, sem.at[6]),
    ]
    load_fin.wait()
    norm = F32(1.0 / math.sqrt(count * EDGE**3))
    for k in range(3):
        for s in range(9):
            p, q = PLACE[s], PLACE[8 - s]
            if p < 8:
                top, left = 288 + 96 * (p // 4) + k * C, (p % 4) * C
            else:
                top, left = 480, k * C
            rows = fin[top : top + C, :].astype(F32)
            one_buf[k * 9 + s] = rows[:, left : left + C] * norm
            rows = fin[q * C : (q + 1) * C, :].astype(F32)
            two_buf[k * 9 + s] = rows[:, (2 - k) * C : (3 - k) * C] * norm
    stores[0].start()
    stores[1].start()
    load_enc.wait()
    stores[2].start()
    load_gfeat.wait()
    stores[3].start()
    for copy in stores:
        copy.wait()


def local(count, *args):
    features, pool, skip, one, two, links, positions, seed = args
    shift = jnp.asarray(shift_matrices(), BF)
    face = jnp.asarray(face_matrix(), BF)
    rows, lanes = SLABS * C, SLABS * PLANE
    dma = pltpu.SemaphoreType.DMA
    rings = count // 32
    hbm = pl.BlockSpec(memory_space=pltpu.HBM)
    field = jax.ShapeDtypeStruct((1, C, EDGE**3), BF)
    weight = jax.ShapeDtypeStruct((27, C, C), F32)
    done = pl.pallas_call(
        functools.partial(kernel, count),
        out_shape=(field, field, jax.ShapeDtypeStruct((512, 128), BF)),
        in_specs=[hbm] * 10,
        out_specs=(hbm,) * 3,
        scratch_shapes=[pltpu.VMEM((1, C, EDGE**3), BF)] * 5
        + [pltpu.VMEM((27, C, C), BF)] * 2
        + [pltpu.VMEM((PLANE + 128, 8 * PLANE), BF), pltpu.VMEM((2 * PLANE, 128), BF)]
        + [
            pltpu.SMEM((1, 6), jnp.int32),
            pltpu.SMEM((1, 3), jnp.int32),
            pltpu.SMEM((1,), jnp.int32),
        ]
        + [pltpu.VMEM((rows, PLANE + 128), BF)] * 4
        + [pltpu.VMEM((9 * C, lanes), BF)] * 2
        + [pltpu.VMEM((8 * C, lanes), BF)] * 2
        + [pltpu.VMEM((96, 256), BF)] * 4
        + [pltpu.VMEM((C, 96), BF)] * 4
        + [pltpu.VMEM((96, lanes), F32)] * 2
        + [pltpu.VMEM((EDGE * C, PLANE), F32)] * 2
        + [pltpu.VMEM((96, lanes), BF)] * 2
        + [pltpu.VMEM((4, 384, 128), BF)] * 3
        + [
            pltpu.VMEM((512, 128), F32),
            pltpu.VMEM((512, 128), BF),
            pltpu.VMEM((32, 16, 128), BF),
            pltpu.VMEM((rings, 16, 128), F32),
            pltpu.VMEM((16, 128), BF),
            pltpu.VMEM((512, 128), BF),
            pltpu.SemaphoreType.REGULAR((2,)),
            dma((10,)),
            dma((3,)),
            dma((8,)),
            dma((8,)),
            dma((1,)),
            dma((1,)),
            dma((1,)),
            dma((1,)),
            dma((1,)),
            dma((1,)),
        ],
        compiler_params=pltpu.CompilerParams(
            collective_id=0, has_side_effects=True, vmem_limit_bytes=64 * 2**20
        ),
        cost_estimate=pl.CostEstimate(
            flops=4_000_000_000, bytes_accessed=3_000_000, transcendentals=300_000
        ),
    )(features, pool, skip, one, two, shift, face, links, positions, seed)
    return pl.pallas_call(
        functools.partial(write_out, count),
        out_shape=(field, field, weight, weight),
        in_specs=[hbm] * 3,
        out_specs=(hbm,) * 4,
        scratch_shapes=[pltpu.VMEM((1, C, EDGE**3), BF)] * 2
        + [pltpu.VMEM((512, 128), BF)]
        + [pltpu.VMEM((27, C, C), F32)] * 2
        + [dma((7,))],
        compiler_params=pltpu.CompilerParams(vmem_limit_bytes=64 * 2**20),
        cost_estimate=pl.CostEstimate(flops=0, bytes_accessed=2_000_000, transcendentals=0),
    )(*done)


def solution(mesh):
    both = ("blocks", "section")
    in_specs = (
        P(both, None, None),
        P(both, None, None),
        P(both, None, None),
        P(),
        P(),
        P(both, None),
        P(both, None),
        P(),
    )
    out_specs = (P(both, None, None), P(both, None, None), P(), P())
    return jax.shard_map(
        functools.partial(local, mesh.size),
        mesh=mesh,
        in_specs=in_specs,
        out_specs=out_specs,
        check_vma=False,
    )
```
